512 devices in a mesh: slab: 128 (over y, z, core), sub: 4 (over x).
Axes of the slice: x: 4, y: 4, z: 16, core: 2. Of those that a mesh axis runs over, the one named last changes fastest.
Arguments:
- covariates: bfloat16 [1048576, 128], P(('slab', 'sub')), may hold values from -6 to 6
- partition_slot: int32 [2, 1048576], P(None, ('slab', 'sub')), may hold values from 0 to 2047, as said below
- in_weight: bfloat16 [128, 256], replicated, may hold values from -0.5 to 0.5
- in_bias: float32 [256], replicated, may hold values from -3 to 3
- out_weight: bfloat16 [3, 256], replicated, may hold values from -0.375 to 0.375
- out_bias: float32 [3], replicated, may hold values from -2.5 to 2.5
- gradients: float32 [2, 2, 1048576], P(None, None, ('slab', 'sub')), may hold values from -6 to 6
- areas: float32 [1048576], P(('slab', 'sub')), may hold values from 0.02 to 0.2
- corners: int32 [2, 3, 1048576], P(None, None, ('slab', 'sub')), may hold values from 0 to 127, as said below
- tile_rows: int32 [8192], P(('slab', 'sub')), may hold values from 0 to 2047, as said below
- tile_cols: int32 [8192], P(('slab', 'sub')), may hold values from 0 to 2047, as said below
- probe: bfloat16 [64, 262144], P(None, ('slab', 'sub')), may hold values from -6 to 6
Outputs:
- applied: float32 [64, 262144], P(None, ('slab', 'sub'))
The draws below stay inside these ranges and needn't reach their ends.
Inputs may be any that keep to these rules, and one draw needn't show every extreme that they name: The pairs (2048 * partition_slot[0,r] + partition_slot[1,r]) form a permutation of the rows; of the 2048 raster rows of each device, equally many go to every device; partition_slot[0] is below the number of devices and partition_slot[1] below 2048. `corners`: an element's three row positions are distinct, and so are its three column positions. `tile_rows`: the 16 tiles of a device name row blocks of devices with its own slab index; at most 8 of them name blocks of any one device, and in every slab exactly 8 of the tiles of each device name blocks of one common device. `tile_cols`: each tile names a column block of a device whose slab index differs from that of the tile's device by at most one.
All inputs are finite; a program needn't handle non-finite values.
Results may differ from the reference program's by a relative error of at most 0.0053.
Values may be sent and summed in bfloat16 or wider, within the bound.
No kernel may reach another device: no remote copies, remote signals or barrier semaphores. Data moves between devices by JAX's collectives and lax.ppermute only.
A program may use at most 64 MiB of HBM per device.

```python
import math
import jax
import jax.numpy as jnp
from jax import lax

COV = 128
HID = 256
COLS = 64
BLK = 128
ELT = 128
ELEM_DEV = 2048
BLK_DEV = 4
ELEMENTS = 1048576
TILE_DEV = 16
TILES = 8192
NODES = 262144
PEERS = 4
SLABS = 128


def permute_rows(key_list, length):

    def single(row_key):
        return jax.random.permutation(row_key, length)
    return jax.vmap(single)(key_list).astype(jnp.int32)


def draw_partition_slot(key, part):
    key = jax.random.fold_in(key, 11)
    device_count = ELEMENTS // ELEM_DEV
    per_peer = ELEM_DEV // device_count
    key_rows, key_slots = jax.random.split(key)
    sender = jnp.arange(device_count, dtype=jnp.int32)[:, None]
    within = jnp.arange(ELEM_DEV, dtype=jnp.int32)[None, :]
    target = jnp.broadcast_to(within // per_peer, (device_count, ELEM_DEV))
    target_local = sender * per_peer + within % per_peer
    shuffles = permute_rows(jax.random.split(key_slots, device_count), ELEM_DEV)
    moved_local = shuffles[target, target_local]
    mixing = permute_rows(jax.random.split(key_rows, device_count), ELEM_DEV)
    target = jnp.take_along_axis(target, mixing, axis=1)
    moved_local = jnp.take_along_axis(moved_local, mixing, axis=1)
    return jnp.stack([target.reshape(-1), moved_local.reshape(-1)]).astype(jnp.int32)


def draw_corners(key, part):
    key = jax.random.fold_in(key, 41)
    key_start, key_first, key_second = jax.random.split(key, 3)
    start = jax.random.randint(key_start, (2, ELEMENTS), 0, BLK)
    first_gap = jax.random.randint(key_first, (2, ELEMENTS), 1, BLK)
    offset = jax.random.randint(key_second, (2, ELEMENTS), 1, BLK - 1)
    second_gap = 1 + (first_gap - 1 + offset) % (BLK - 1)
    stacked = jnp.stack([start, (start + first_gap) % BLK, (start + second_gap) % BLK], axis=1)
    return stacked.astype(jnp.int32)


def draw_tile_rows(key, part):
    key = jax.random.fold_in(key, 21)
    device_count = TILES // TILE_DEV
    slab_of = jnp.arange(device_count, dtype=jnp.int32) // PEERS
    key_hot, key_other, key_mix, key_block = jax.random.split(key, 4)
    busiest = jax.random.randint(key_hot, (SLABS,), 0, PEERS)[slab_of]
    other = jax.random.randint(key_other, (device_count, TILE_DEV), 1, PEERS)
    position = jnp.arange(TILE_DEV, dtype=jnp.int32)[None, :]
    owner_sub = jnp.where(position < TILE_DEV // 2, busiest[:, None], (busiest[:, None] + other) % PEERS)
    mixing = permute_rows(jax.random.split(key_mix, device_count), TILE_DEV)
    owner_sub = jnp.take_along_axis(owner_sub, mixing, axis=1)
    local_block = jax.random.randint(key_block, (device_count, TILE_DEV), 0, BLK_DEV)
    blocks = (slab_of[:, None] * PEERS + owner_sub) * BLK_DEV + local_block
    return blocks.reshape(-1).astype(jnp.int32)


def draw_tile_cols(key, part):
    key = jax.random.fold_in(key, 31)
    device_count = TILES // TILE_DEV
    slab_of = jnp.arange(device_count, dtype=jnp.int32) // PEERS
    key_step, key_sub, key_block = jax.random.split(key, 3)
    slab_step = jax.random.randint(key_step, (device_count, TILE_DEV), -1, 2)
    other_slab = jnp.clip(slab_of[:, None] + slab_step, 0, SLABS - 1)
    other_sub = jax.random.randint(key_sub, (device_count, TILE_DEV), 0, PEERS)
    local_block = jax.random.randint(key_block, (device_count, TILE_DEV), 0, BLK_DEV)
    blocks = (other_slab * PEERS + other_sub) * BLK_DEV + local_block
    return blocks.reshape(-1).astype(jnp.int32)


def block_scale(rng, extent, pieces, smallest, high):
    gain, own = 1.0, jax.random.fold_in(rng, 6)
    for dim, shards_of in pieces:
        draws = jnp.exp(jax.random.uniform(jax.random.fold_in(own, dim), (shards_of,), jnp.float32, smallest / len(pieces), high / len(pieces)))
        gain = gain * jnp.repeat(draws, extent[dim] // shards_of).reshape([-1 if axis == dim else 1 for axis in range(len(extent))])
    return gain


def normal_values(own_key, dims, spread, reach, cuts=(), held_as=jnp.bfloat16):
    drawn = jax.random.normal(own_key, dims, jnp.float32) * spread
    if len(cuts) > 0:
        drawn = block_scale(own_key, dims, cuts, -0.22, 0.18) * drawn
    return jnp.clip(drawn, min=-reach, max=reach).astype(held_as)


def setup_inputs(seed: int = 0) -> dict:
    arg_keys = jax.random.split(jax.random.key(seed), 13)
    covariates = normal_values(arg_keys[0], (ELEMENTS, COV), 1.0, 6.0, ((0, 512),))
    partition_slot = draw_partition_slot(jax.random.fold_in(arg_keys[12], 71), 0)
    in_weight = normal_values(arg_keys[2], (COV, HID), COV ** -0.5, 0.5)
    in_bias = normal_values(arg_keys[3], (HID,), 0.5, 3.0, (), jnp.float32)
    out_weight = normal_values(arg_keys[4], (3, HID), HID ** -0.5, 0.375)
    out_bias = normal_values(arg_keys[5], (3,), 0.5, 2.5, (), jnp.float32)
    gradients = normal_values(arg_keys[6], (2, 2, ELEMENTS), 1.0, 6.0, ((2, 512),), jnp.float32)
    areas = jnp.clip(jnp.exp(math.log(0.2) - 2.3025851 * jax.random.uniform(arg_keys[7], (ELEMENTS,), jnp.float32) ** block_scale(arg_keys[7], (ELEMENTS,), ((0, 512),), -0.2, 0.2)), 0.02, 0.2)
    corners = draw_corners(jax.random.fold_in(arg_keys[12], 71), 0)
    tile_rows = draw_tile_rows(jax.random.fold_in(arg_keys[12], 71), 0)
    tile_cols = draw_tile_cols(jax.random.fold_in(arg_keys[12], 71), 0)
    probe = normal_values(arg_keys[11], (COLS, NODES), 1.0, 6.0, ((1, 512),))
    return {"covariates": covariates, "partition_slot": partition_slot, "in_weight": in_weight, "in_bias": in_bias, "out_weight": out_weight, "out_bias": out_bias, "gradients": gradients, "areas": areas, "corners": corners, "tile_rows": tile_rows, "tile_cols": tile_cols, "probe": probe}


def features_to_params(feature_rows, in_weight, in_bias, out_weight, out_bias):
    pre_act = jnp.dot(feature_rows, in_weight, preferred_element_type=jnp.float32) + in_bias
    hidden = jax.nn.gelu(pre_act, approximate=True).astype(jnp.bfloat16)
    outputs = lax.dot_general(out_weight, hidden, (((1,), (1,)), ((), ())), preferred_element_type=jnp.float32)
    return outputs + out_bias[:, None]


def element_matrices(params, gradients, areas):
    kappa_sq = jnp.exp(params[0])
    aniso_scale = jnp.exp(params[1])
    coupling = 0.9 * jnp.tanh(params[2])
    grad_x = [gradients[0, 0], gradients[0, 1], -(gradients[0, 0] + gradients[0, 1])]
    grad_y = [gradients[1, 0], gradients[1, 1], -(gradients[1, 0] + gradients[1, 1])]
    rows_out = []
    for corner_a in range(3):
        matrix_row = []
        for corner_b in range(3):
            stiffness = grad_x[corner_a] * grad_x[corner_b] + grad_y[corner_a] * grad_y[corner_b]
            stiffness = stiffness + coupling * (grad_x[corner_a] * grad_y[corner_b] + grad_y[corner_a] * grad_x[corner_b])
            mass_term = kappa_sq * (2.0 if corner_a == corner_b else 1.0)
            matrix_row.append(areas * (aniso_scale * stiffness + mass_term))
        rows_out.append(jnp.stack(matrix_row))
    return jnp.stack(rows_out).astype(jnp.bfloat16)


def reference(covariates, partition_slot, in_weight, in_bias, out_weight, out_bias, gradients, areas, corners, tile_rows, tile_cols, probe):
    blocks = covariates.reshape(ELEMENTS // ELEM_DEV, ELEM_DEV, COV)

    def block_params(feature_rows):
        return features_to_params(feature_rows, in_weight, in_bias, out_weight, out_bias)

    per_block = lax.map(block_params, blocks)
    raster = jnp.transpose(per_block, (1, 0, 2)).reshape(3, ELEMENTS)
    global_slot = (partition_slot[0] * ELEM_DEV + partition_slot[1]).astype(jnp.int32)
    params = jnp.zeros((3, ELEMENTS), raster.dtype).at[:, global_slot].set(raster)
    element_k = element_matrices(params, gradients, areas)
    k_tiles = element_k.reshape(3, 3, TILES, ELT).transpose(2, 0, 1, 3)
    pos_tiles = corners.reshape(2, 3, TILES, ELT).transpose(2, 0, 1, 3)

    def add_tile(result, tile_items):
        k_here, pos_here, row_block, col_block = tile_items
        rows_idx = jnp.broadcast_to(pos_here[0][:, None, :], (3, 3, ELT))
        cols_idx = jnp.broadcast_to(pos_here[1][None, :, :], (3, 3, ELT))
        assembled = jnp.zeros((BLK, BLK), jnp.float32).at[rows_idx, cols_idx].add(k_here.astype(jnp.float32))
        assembled = assembled.astype(jnp.bfloat16)
        column_start = (col_block * BLK).astype(jnp.int32)
        block_cols = lax.dynamic_slice(probe, (jnp.int32(0), column_start), (COLS, BLK))
        contrib = lax.dot_general(block_cols, assembled, (((1,), (1,)), ((), ())), preferred_element_type=jnp.float32)
        row_start = (row_block * BLK).astype(jnp.int32)
        current = lax.dynamic_slice(result, (jnp.int32(0), row_start), (COLS, BLK))
        return lax.dynamic_update_slice(result, current + contrib, (jnp.int32(0), row_start)), None

    applied, unused = lax.scan(add_tile, jnp.zeros((COLS, NODES), jnp.float32), (k_tiles, pos_tiles, tile_rows, tile_cols))
    return applied
```

```python
import jax
import jax.numpy as jnp
from jax import lax
from jax.experimental import pallas as pl
from jax.experimental.pallas import tpu as pltpu
from jax.sharding import PartitionSpec as P

BLK = 128
CHUNKS = 16
RANKS = 16
FIELDS = 8
SLOTS = 32
TILES_SLAB = 64
SUBS = 4
BLK_DEV = 4
COLS = 64
PAIRS = ((0, 0), (0, 1), (0, 2), (1, 1), (1, 2), (2, 2))
PAIR_OF = {(a, b): PAIRS.index((min(a, b), max(a, b))) for a in range(3) for b in range(3)}
NT = (((1,), (1,)), ((), ()))
VMEM = pl.BlockSpec(memory_space=pltpu.VMEM)
SMEM = pl.BlockSpec(memory_space=pltpu.SMEM)
F32 = jnp.float32
BF16 = jnp.bfloat16


def call(kernel, out_shape, in_specs, out_specs, scratch, flops, nbytes):
    return pl.pallas_call(
        kernel,
        out_shape=out_shape,
        in_specs=in_specs,
        out_specs=out_specs,
        scratch_shapes=scratch,
        compiler_params=pltpu.CompilerParams(vmem_limit_bytes=40 * 1024 * 1024),
        cost_estimate=pl.CostEstimate(flops=flops, bytes_accessed=nbytes, transcendentals=0),
    )


def lanes(chunk):
    return slice(chunk * BLK, (chunk + 1) * BLK)


def pack_kernel(grad_ref, area_ref, corner_ref, rows_ref, cols_ref, out_ref):
    out_ref[0:1, :] = grad_ref[0, 0:1, :]
    out_ref[1:2, :] = grad_ref[0, 1:2, :]
    out_ref[2:3, :] = grad_ref[1, 0:1, :]
    out_ref[3:4, :] = grad_ref[1, 1:2, :]
    out_ref[4:5, :] = area_ref[...]
    for side in range(2):
        packed = (
            corner_ref[side, 0:1, :]
            + corner_ref[side, 1:2, :] * BLK
            + corner_ref[side, 2:3, :] * (BLK * BLK)
        )
        out_ref[5 + side : 6 + side, :] = packed.astype(F32)
    out_ref[7:8, :] = jnp.zeros((1, out_ref.shape[1]), F32)
    out_ref[7:8, 0:16] = rows_ref[...].astype(F32)
    out_ref[7:8, 16:32] = cols_ref[...].astype(F32)


def route_kernel(cov_ref, slot_ref, w1_ref, b1_ref, w2_ref, b2_ref, out_ref, hot_ref, val_ref, par_ref):
    rows = 256
    for part in range(cov_ref.shape[0] // rows):
        here = slice(part * rows, (part + 1) * rows)
        pre_act = (
            jnp.dot(cov_ref[here, :], w1_ref[...], preferred_element_type=F32) + b1_ref[...]
        )
        hidden = jax.nn.gelu(pre_act, approximate=True).astype(BF16)
        par_ref[:, here] = (
            lax.dot_general(w2_ref[...], hidden, NT, preferred_element_type=F32) + b2_ref[...]
        )
    slab_iota = lax.broadcasted_iota(jnp.int32, (BLK, BLK), 0)
    lane_iota = lax.broadcasted_iota(jnp.int32, (BLK, BLK), 1)
    for chunk in range(CHUNKS):
        slab = slot_ref[0:1, lanes(chunk)] >> 2
        hot_ref[:, lanes(chunk)] = jnp.where(slab_iota == slab, 1.0, 0.0).astype(BF16)
    earlier = jnp.concatenate(
        [jnp.where(slab_iota < lane_iota, 1.0, 0.0).astype(BF16), jnp.ones((BLK, BLK), BF16)], axis=1
    )
    rank_iota = lax.broadcasted_iota(jnp.int32, (RANKS, BLK), 0).astype(F32)
    seen = jnp.zeros((BLK, BLK), F32)
    for chunk in range(CHUNKS):
        hot = hot_ref[:, lanes(chunk)]
        counts = jnp.dot(hot, earlier, preferred_element_type=F32)
        rank = jnp.sum(hot.astype(F32) * (counts[:, :BLK] + seen), axis=0, keepdims=True)
        seen = seen + counts[:, BLK:]
        params = par_ref[:, lanes(chunk)]
        high = params.astype(BF16).astype(F32)
        low = params - high
        device = slot_ref[0:1, lanes(chunk)]
        place = slot_ref[1:2, lanes(chunk)]
        tile = ((device & 3) * 16 + (place >> 7)).astype(F32)
        lane = (place & 127).astype(F32)
        values = []
        for f in range(3):
            values += [high[f : f + 1], low[f : f + 1]]
        values += [tile, lane]
        mine = rank_iota == rank
        val_ref[:, lanes(chunk)] = jnp.concatenate(
            [jnp.where(mine, v, 0.0).astype(BF16) for v in values], axis=0
        )
    out_ref[...] = lax.dot_general(hot_ref[...], val_ref[...], NT, preferred_element_type=F32)


def window_kernel(meta_ref, elem_ref, before_ref, own_ref, after_ref, tid_ref, geo_ref, pos_ref, xg_ref, info_ref, raw_ref):
    me = lax.axis_index("sub")
    base = (lax.axis_index("slab") - 1) * (SUBS * BLK_DEV)
    tid_ref[...] = jnp.full(tid_ref.shape, -1.0, F32)

    def find(t, n):
        u, k = t // 16, t % 16
        row = meta_ref[u, k]
        owned = (row // BLK_DEV) % SUBS == me

        @pl.when(owned)
        def _():
            info_ref[0, n] = row % BLK_DEV
            info_ref[1, n] = meta_ref[u, 16 + k] - base
            info_ref[2, n] = t
            tid_ref[pl.ds(n, 1), :] = jnp.full((1, BLK), t, jnp.int32).astype(F32)

        return n + owned.astype(jnp.int32)

    count = lax.fori_loop(0, TILES_SLAB, find, jnp.int32(0))
    info_ref[0, SLOTS] = count
    node_iota = lax.broadcasted_iota(jnp.int32, (BLK, BLK), 0)

    def gather(n, carry):
        t, col = info_ref[2, n], info_ref[1, n]
        u, k = t // 16, t % 16
        rows = elem_ref[u, :, pl.ds(pl.multiple_of(k * BLK, BLK), BLK)]
        for f in range(7):
            raw_ref[f, pl.ds(n, 1), :] = rows[f : f + 1]
        packed = rows[6:7].astype(jnp.int32)
        hot = jnp.concatenate(
            [
                jnp.where(node_iota == ((packed >> (7 * b)) & 127), 1.0, 0.0).astype(BF16)
                for b in range(3)
            ],
            axis=1,
        )
        step, s, blk = col // 16, (col // 4) % 4, col % 4
        where = pl.ds(pl.multiple_of(blk * BLK, BLK), BLK)

        def store(ref):
            def _():
                xg_ref[n] = jnp.dot(ref[s, :, where], hot, preferred_element_type=F32).astype(BF16)

            return _

        pl.when(step == 0)(store(before_ref))
        pl.when(step == 1)(store(own_ref))
        pl.when(step == 2)(store(after_ref))
        return carry

    lax.fori_loop(0, count, gather, jnp.int32(0))
    grad_x = [raw_ref[0], raw_ref[1]]
    grad_x.append(-(grad_x[0] + grad_x[1]))
    grad_y = [raw_ref[2], raw_ref[3]]
    grad_y.append(-(grad_y[0] + grad_y[1]))
    for i, (a, b) in enumerate(PAIRS):
        geo_ref[i] = grad_x[a] * grad_x[b] + grad_y[a] * grad_y[b]
        geo_ref[6 + i] = grad_x[a] * grad_y[b] + grad_y[a] * grad_x[b]
    geo_ref[12] = raw_ref[4]
    row_packed = raw_ref[5].astype(jnp.int32)
    for a in range(3):
        pos_ref[a] = (row_packed >> (7 * a)) & 127


def apply_kernel(info_ref, got_ref, tid_ref, geo_ref, pos_ref, xg_ref, out_ref, hot_ref, val_ref, k_ref, turned_ref):
    lane_iota = lax.broadcasted_iota(jnp.int32, (BLK, BLK), 0).astype(F32)
    tiles = tid_ref[...]
    found = jnp.zeros((6 * SLOTS, BLK), F32)
    for u in range(SUBS):
        turned_ref[...] = got_ref[u].T
        for k in range(RANKS):
            rows = [turned_ref[f * RANKS + k : f * RANKS + k + 1, :] for f in range(FIELDS)]
            mine = tiles == rows[6]
            val_ref[:, lanes(k)] = jnp.concatenate(
                [jnp.where(mine, rows[f], 0.0).astype(BF16) for f in range(6)], axis=0
            )
            hot_ref[:, lanes(k)] = jnp.where(lane_iota == rows[7], 1.0, 0.0).astype(BF16)
        found = found + lax.dot_general(val_ref[...], hot_ref[...], NT, preferred_element_type=F32)
    params = [
        found[2 * f * SLOTS : (2 * f + 1) * SLOTS] + found[(2 * f + 1) * SLOTS : (2 * f + 2) * SLOTS]
        for f in range(3)
    ]
    kappa_sq = jnp.exp(params[0])
    scale = jnp.exp(params[1])
    coupling = 0.9 * jnp.tanh(params[2])
    area = geo_ref[12]
    for i, (a, b) in enumerate(PAIRS):
        mass = kappa_sq * (2.0 if a == b else 1.0)
        stiffness = scale * (geo_ref[i] + coupling * geo_ref[6 + i])
        k_ref[i] = (area * (stiffness + mass)).astype(BF16).astype(F32)
    out_ref[...] = jnp.zeros(out_ref.shape, F32)
    node_iota = lax.broadcasted_iota(jnp.int32, (BLK, BLK), 0)

    def add(n, carry):
        k = [k_ref[i, pl.ds(n, 1), :] for i in range(6)]
        x = xg_ref[n].astype(F32)
        xs = [x[:, lanes(b)] for b in range(3)]
        ys = []
        hots = []
        for a in range(3):
            y = k[PAIR_OF[a, 0]] * xs[0] + k[PAIR_OF[a, 1]] * xs[1] + k[PAIR_OF[a, 2]] * xs[2]
            ys.append(y.astype(BF16))
            hots.append(jnp.where(node_iota == pos_ref[a, pl.ds(n, 1), :], 1.0, 0.0).astype(BF16))
        part = lax.dot_general(
            jnp.concatenate(ys, axis=1), jnp.concatenate(hots, axis=1), NT, preferred_element_type=F32
        )
        where = pl.ds(pl.multiple_of(info_ref[0, n] * BLK, BLK), BLK)
        out_ref[:, where] = out_ref[:, where] + part
        return carry

    lax.fori_loop(0, info_ref[0, SLOTS], add, jnp.int32(0))


def shared(block):
    copies = jnp.broadcast_to(block[None], (SUBS, *block.shape))
    return lax.all_to_all(copies, "sub", split_axis=0, concat_axis=0, tiled=True)


def local(
    covariates,
    partition_slot,
    in_weight,
    in_bias,
    out_weight,
    out_bias,
    gradients,
    areas,
    corners,
    tile_rows,
    tile_cols,
    probe,
):
    elements = areas.shape[0]
    slabs = lax.axis_size("slab")
    sds = jax.ShapeDtypeStruct
    packed = call(
        pack_kernel, sds((8, elements), F32), [VMEM] * 5, VMEM, (), 10000, 200000
    )(gradients, areas[None], corners, tile_rows[None], tile_cols[None])
    routed = call(
        route_kernel,
        sds((BLK, BLK), F32),
        [VMEM] * 6,
        VMEM,
        [pltpu.VMEM((BLK, elements), BF16), pltpu.VMEM((BLK, elements), BF16), pltpu.VMEM((3, elements), F32)],
        400_000_000,
        1_000_000,
    )(covariates, partition_slot, in_weight, in_bias[None], out_weight, out_bias[:, None])
    arrived = lax.all_to_all(routed, "slab", split_axis=0, concat_axis=0, tiled=True)

    elem = shared(packed)
    own = shared(probe)
    up = [(i, i + 1) for i in range(slabs - 1)]
    before = lax.ppermute(own, "slab", up)
    after = lax.ppermute(own, "slab", [(j, i) for i, j in up])
    meta = elem[:, 7, :32].astype(jnp.int32)
    tid, geo, pos, xg, info = call(
        window_kernel,
        (
            sds((SLOTS, BLK), F32),
            sds((13, SLOTS, BLK), F32),
            sds((3, SLOTS, BLK), jnp.int32),
            sds((SLOTS, COLS, 3 * BLK), BF16),
            sds((3, SLOTS + 1), jnp.int32),
        ),
        [SMEM, VMEM, VMEM, VMEM, VMEM],
        (VMEM, VMEM, VMEM, VMEM, SMEM),
        [pltpu.VMEM((7, SLOTS, BLK), F32)],
        400_000_000,
        3_000_000,
    )(meta, elem, before, own, after)
    got = shared(arrived.astype(BF16)).astype(F32)
    return call(
        apply_kernel,
        sds((COLS, probe.shape[1]), F32),
        [SMEM] + [VMEM] * 5,
        VMEM,
        [
            pltpu.VMEM((BLK, RANKS * BLK), BF16),
            pltpu.VMEM((6 * SLOTS, RANKS * BLK), BF16),
            pltpu.VMEM((6, SLOTS, BLK), F32),
            pltpu.VMEM((BLK, BLK), F32),
        ],
        1_000_000_000,
        3_000_000,
    )(info, got, tid, geo, pos, xg)


def solution(mesh):
    placed = (
        P(("slab", "sub"), None),
        P(None, ("slab", "sub")),
        P(),
        P(),
        P(),
        P(),
        P(None, None, ("slab", "sub")),
        P(("slab", "sub")),
        P(None, None, ("slab", "sub")),
        P(("slab", "sub")),
        P(("slab", "sub")),
        P(None, ("slab", "sub")),
    )
    return jax.shard_map(
        local, mesh=mesh, in_specs=placed, out_specs=P(None, ("slab", "sub")), check_vma=False
    )
```

```python
import jax
import jax.numpy as jnp
from jax import lax
from jax.experimental import pallas as pl
from jax.experimental.pallas import tpu as pltpu
from jax.sharding import PartitionSpec as P

BLK = 128
CHUNKS = 16
RANKS = 16
FIELDS = 8
SLOTS = 32
TILES_SLAB = 64
TILE_DEV = 16
SUBS = 4
BLK_DEV = 4
COLS = 64
PAIRS = ((0, 0), (0, 1), (0, 2), (1, 1), (1, 2), (2, 2))
PAIR_OF = {(a, b): PAIRS.index((min(a, b), max(a, b))) for a in range(3) for b in range(3)}
NT = (((1,), (1,)), ((), ()))
VMEM = pl.BlockSpec(memory_space=pltpu.VMEM)
SMEM = pl.BlockSpec(memory_space=pltpu.SMEM)
F32 = jnp.float32
BF16 = jnp.bfloat16


HBM = pl.BlockSpec(memory_space=pltpu.HBM)
ANY = pl.BlockSpec(memory_space=pl.ANY)
ELEM_FIELDS = 32
SEND_ROWS = 256


def call(kernel, out_shape, in_specs, out_specs, scratch, flops, nbytes, vmem=40):
    return pl.pallas_call(
        kernel,
        out_shape=out_shape,
        in_specs=in_specs,
        out_specs=out_specs,
        scratch_shapes=scratch,
        compiler_params=pltpu.CompilerParams(vmem_limit_bytes=vmem * 1024 * 1024),
        cost_estimate=pl.CostEstimate(flops=flops, bytes_accessed=nbytes, transcendentals=0),
    )


def lanes(chunk):
    return slice(chunk * BLK, (chunk + 1) * BLK)


def parts(x, n):
    out = []
    for _ in range(n - 1):
        out.append(x.astype(BF16).astype(F32))
        x = x - out[-1]
    return out + [x]


def pack_elements(grad_ref, area_ref, corner_ref, rows_ref, cols_ref, send_ref, meta_ref):
    meta_ref[...] = jnp.zeros(meta_ref.shape, F32)
    for i, ref in enumerate((rows_ref, cols_ref)):
        meta_ref[2 * i : 2 * i + 1, 0:TILE_DEV] = (ref[...] >> 4).astype(F32)
        meta_ref[2 * i + 1 : 2 * i + 2, 0:TILE_DEV] = (ref[...] & 15).astype(F32)
    for q in range(4):
        here = slice(q * 512, (q + 1) * 512)
        fields = []
        for i in range(2):
            for j in range(2):
                fields += parts(grad_ref[i, j : j + 1, here], 3)
        fields += parts(area_ref[:, here], 3)
        for side in range(2):
            for a in range(3):
                fields.append(corner_ref[a, side : side + 1, here].astype(F32))
        fields += [meta_ref[...], jnp.zeros((ELEM_FIELDS - 29, 512), F32)]
        top = COLS + q * ELEM_FIELDS
        send_ref[top : top + ELEM_FIELDS, :] = jnp.concatenate(fields, axis=0).astype(BF16)


def route_kernel(
    cov_hbm, slot_hbm, w1_hbm, b1_hbm, w2_hbm, b2_ref, grad_hbm, area_hbm, corner_hbm, probe_hbm, rows_ref, cols_ref,
    out_ref, send_ref,
    cov_ref, slot_ref, w1_ref, b1_ref, w2_ref, grad_ref, area_ref, corner_ref, hot_ref, count_ref, val_ref, par_ref, meta_ref, sem,
):
    pairs = (
        (slot_hbm, slot_ref), (cov_hbm, cov_ref), (w1_hbm, w1_ref), (b1_hbm, b1_ref), (w2_hbm, w2_ref),
        (grad_hbm, grad_ref), (area_hbm, area_ref), (corner_hbm, corner_ref),
        (probe_hbm, send_ref.at[0:COLS]),
    )
    copies = [pltpu.make_async_copy(s, d, sem.at[i]) for i, (s, d) in enumerate(pairs)]
    for c in copies:
        c.start()
    slab_iota = lax.broadcasted_iota(jnp.int32, (BLK, BLK), 0)
    lane_iota = lax.broadcasted_iota(jnp.int32, (BLK, BLK), 1)
    earlier = jnp.concatenate(
        [jnp.where(slab_iota < lane_iota, 1.0, 0.0).astype(BF16), jnp.ones((BLK, BLK), BF16)], axis=1
    )
    copies[0].wait()
    for chunk in range(CHUNKS):
        slab = slot_ref[0:1, lanes(chunk)] >> 2
        hot_ref[:, lanes(chunk)] = jnp.where(slab_iota == slab, 1.0, 0.0).astype(BF16)
    rank_iota = lax.broadcasted_iota(jnp.int32, (RANKS, BLK), 0).astype(F32)
    seen = jnp.zeros((BLK, BLK), F32)
    for chunk in range(CHUNKS):
        hot = hot_ref[:, lanes(chunk)]
        counts = jnp.dot(hot, earlier, preferred_element_type=F32)
        rank = jnp.sum(hot.astype(F32) * (counts[:, :BLK] + seen), axis=0, keepdims=True)
        seen = seen + counts[:, BLK:]
        count_ref[:, lanes(chunk)] = rank
    for c in copies[1:5]:
        c.wait()
    rows = 256
    for part in range(cov_ref.shape[0] // rows):
        here = slice(part * rows, (part + 1) * rows)
        pre_act = jnp.dot(cov_ref[here, :], w1_ref[...], preferred_element_type=F32) + b1_ref[...]
        hidden = jax.nn.gelu(pre_act, approximate=True).astype(BF16)
        par_ref[:, here] = lax.dot_general(w2_ref[...], hidden, NT, preferred_element_type=F32)
    for chunk in range(CHUNKS):
        device = slot_ref[0:1, lanes(chunk)]
        place = slot_ref[1:2, lanes(chunk)]
        tile = ((device & 3) * 16 + (place >> 7)).astype(F32)
        lane = (place & 127).astype(F32)
        values = []
        for f in range(3):
            values += parts(par_ref[f : f + 1, lanes(chunk)] + b2_ref[f], 2)
        values += [tile, lane]
        mine = rank_iota == count_ref[:, lanes(chunk)]
        val_ref[:, lanes(chunk)] = jnp.concatenate(
            [jnp.where(mine, v, 0.0).astype(BF16) for v in values], axis=0
        )
    out_ref[...] = lax.dot_general(hot_ref[...], val_ref[...], NT, preferred_element_type=F32).astype(out_ref.dtype)
    for c in copies[5:]:
        c.wait()
    send_ref[COLS + 4 * ELEM_FIELDS :, :] = jnp.zeros((SEND_ROWS - COLS - 4 * ELEM_FIELDS, 512), BF16)
    pack_elements(grad_ref, area_ref, corner_ref, rows_ref, cols_ref, send_ref, meta_ref)


def list_kernel(all_ref, tid_ref, geo_ref, pos_ref, info_ref, raw_ref, ints_ref, meta_ref, sem):
    me = lax.axis_index("sub")
    base = (lax.axis_index("slab") - 1) * (SUBS * BLK_DEV)
    for u in range(SUBS):
        coded = all_ref[u, COLS : COLS + ELEM_FIELDS, 0:BLK].astype(F32)
        for i in range(2):
            whole = coded[21 + 2 * i : 22 + 2 * i] * 16.0 + coded[22 + 2 * i : 23 + 2 * i]
            ints_ref[4 * i + u : 4 * i + u + 1, :] = whole.astype(jnp.int32)
    copy = pltpu.make_async_copy(ints_ref, meta_ref, sem.at[0])
    copy.start()
    tid_ref[...] = jnp.full(tid_ref.shape, -1.0, F32)
    raw_ref[...] = jnp.zeros(raw_ref.shape, F32)
    for n in range(SLOTS):
        info_ref[0, n] = 0
        info_ref[1, n] = SUBS * BLK_DEV

    copy.wait()

    def find(t, n):
        u, k = t // 16, t % 16
        row = meta_ref[u, k]
        owned = (row // BLK_DEV) % SUBS == me

        @pl.when(owned)
        def _():
            info_ref[0, n] = row % BLK_DEV
            info_ref[1, n] = meta_ref[4 + u, k] - base
            tid_ref[pl.ds(n, 1), :] = jnp.full((1, BLK), t, jnp.int32).astype(F32)
            top = pl.ds(pl.multiple_of(COLS + (k // 4) * ELEM_FIELDS, 32), ELEM_FIELDS)
            here = pl.ds(pl.multiple_of((k % 4) * BLK, BLK), BLK)
            rows = all_ref[u, top, here].astype(F32)
            for f in range(5):
                raw_ref[f, pl.ds(n, 1), :] = rows[3 * f : 3 * f + 1] + rows[3 * f + 1 : 3 * f + 2] + rows[3 * f + 2 : 3 * f + 3]
            for f in range(6):
                raw_ref[5 + f, pl.ds(n, 1), :] = rows[15 + f : 16 + f]

        return n + owned.astype(jnp.int32)

    info_ref[0, SLOTS] = lax.fori_loop(0, TILES_SLAB, find, jnp.int32(0))
    grad_x = [raw_ref[0], raw_ref[1]]
    grad_x.append(-(grad_x[0] + grad_x[1]))
    grad_y = [raw_ref[2], raw_ref[3]]
    grad_y.append(-(grad_y[0] + grad_y[1]))
    for i, (a, b) in enumerate(PAIRS):
        geo_ref[i] = grad_x[a] * grad_x[b] + grad_y[a] * grad_y[b]
        geo_ref[6 + i] = grad_x[a] * grad_y[b] + grad_y[a] * grad_x[b]
    geo_ref[12] = raw_ref[4]
    for a in range(6):
        pos_ref[a] = raw_ref[5 + a].astype(jnp.int32)


def apply_kernel(
    info_ref, got_ref, tid_ref, geo_ref, pos_ref, before_hbm, own_hbm, after_hbm,
    out_ref, hot_ref, val_ref, k_ref, turned_ref, x_ref, acc_ref, sem,
):
    copies = [
        pltpu.make_async_copy(src, x_ref.at[4 * i : 4 * i + 4], sem.at[i])
        for i, src in enumerate((before_hbm, own_hbm, after_hbm))
    ]
    for c in copies:
        c.start()
    lane_iota = lax.broadcasted_iota(jnp.int32, (BLK, BLK), 0).astype(F32).astype(BF16)
    one, zero = jnp.ones((), BF16), jnp.zeros((), BF16)
    tiles = tid_ref[...].astype(BF16)
    found = jnp.zeros((6 * SLOTS, BLK), F32)
    for u in range(SUBS):
        turned_ref[...] = got_ref[u].astype(F32).T
        for k in range(RANKS):
            rows = [
                jnp.broadcast_to(turned_ref[f * RANKS + k : f * RANKS + k + 1, :], (16, BLK)).astype(BF16)
                for f in range(FIELDS)
            ]
            twice = [jnp.concatenate([r, r], axis=0) for r in rows[:7]]
            mine = tiles == twice[6]
            val_ref[:, lanes(k)] = jnp.concatenate([jnp.where(mine, twice[f], zero) for f in range(6)], axis=0)
            hot_ref[:, lanes(k)] = jnp.where(lane_iota == jnp.concatenate([rows[7]] * 8, axis=0), one, zero)
        found = found + lax.dot_general(val_ref[...], hot_ref[...], NT, preferred_element_type=F32)
    params = [
        found[2 * f * SLOTS : (2 * f + 1) * SLOTS] + found[(2 * f + 1) * SLOTS : (2 * f + 2) * SLOTS]
        for f in range(3)
    ]
    kappa_sq = jnp.exp(params[0])
    scale = jnp.exp(params[1])
    coupling = 0.9 * jnp.tanh(params[2])
    area = geo_ref[12]
    for i, (a, b) in enumerate(PAIRS):
        mass = kappa_sq * (2.0 if a == b else 1.0)
        stiffness = scale * (geo_ref[i] + coupling * geo_ref[6 + i])
        k_ref[i] = (area * (stiffness + mass)).astype(BF16).astype(F32)
    acc_ref[...] = jnp.zeros(acc_ref.shape, F32)
    for c in copies:
        c.wait()

    def tile_part(n):
        col = info_ref[1, n]
        where = pl.ds(pl.multiple_of((col % 4) * BLK, BLK), BLK)
        x = x_ref[col // 4, :, where].astype(F32)
        k = [k_ref[i, pl.ds(n, 1), :] for i in range(6)]
        xs = [
            jnp.take_along_axis(x, jnp.broadcast_to(pos_ref[3 + b, pl.ds(n, 1), :], (COLS, BLK)), axis=1)
            for b in range(3)
        ]
        ys = []
        hots = []
        for a in range(3):
            y = k[PAIR_OF[a, 0]] * xs[0] + k[PAIR_OF[a, 1]] * xs[1] + k[PAIR_OF[a, 2]] * xs[2]
            ys.append(y.astype(BF16))
            row = jnp.broadcast_to(pos_ref[a, pl.ds(n, 1), :].astype(F32), (16, BLK)).astype(BF16)
            hots.append(jnp.where(lane_iota == jnp.concatenate([row] * 8, axis=0), one, zero))
        return lax.dot_general(
            jnp.concatenate(ys, axis=1), jnp.concatenate(hots, axis=1), NT, preferred_element_type=F32
        )

    def add(group, carry):
        done = [tile_part(group * UNROLL + i) for i in range(UNROLL)]
        for i in range(UNROLL):
            block = info_ref[0, group * UNROLL + i]
            acc_ref[block] = acc_ref[block] + done[i]
        return carry

    lax.fori_loop(0, (info_ref[0, SLOTS] + UNROLL - 1) // UNROLL, add, jnp.int32(0))
    for block in range(BLK_DEV):
        out_ref[:, lanes(block)] = acc_ref[block]


UNROLL = 4


def shared(block):
    copies = jnp.broadcast_to(block[None], (SUBS, *block.shape))
    return lax.all_to_all(copies, "sub", split_axis=0, concat_axis=0, tiled=True)


def local(
    covariates,
    partition_slot,
    in_weight,
    in_bias,
    out_weight,
    out_bias,
    gradients,
    areas,
    corners,
    tile_rows,
    tile_cols,
    probe,
):
    elements = areas.shape[0]
    slabs = lax.axis_size("slab")
    sds = jax.ShapeDtypeStruct
    vm = pltpu.VMEM
    routed, send = call(
        route_kernel,
        (sds((BLK, BLK), F32), sds((SEND_ROWS, 512), BF16)),
        [HBM] * 5 + [SMEM] + [HBM] * 4 + [VMEM] * 2,
        (VMEM, VMEM),
        [
            vm(covariates.shape, BF16),
            vm(partition_slot.shape, jnp.int32),
            vm(in_weight.shape, BF16),
            vm((1, in_bias.shape[0]), F32),
            vm(out_weight.shape, BF16),
            vm(gradients.shape, F32),
            vm((1, elements), F32),
            vm((3, 2, elements), jnp.int32),
            vm((BLK, elements), BF16),
            vm((1, elements), F32),
            vm((BLK, elements), BF16),
            vm((3, elements), F32),
            vm((8, 512), F32),
            pltpu.SemaphoreType.DMA((9,)),
        ],
        400_000_000,
        1_000_000,
        60,
    )(
        covariates, partition_slot, in_weight, in_bias[None], out_weight, out_bias,
        gradients, areas[None], corners.transpose(1, 0, 2), probe, tile_rows[None], tile_cols[None],
    )
    everything = lax.all_gather(send, "sub")
    arrived = lax.all_to_all(routed, "slab", split_axis=0, concat_axis=0, tiled=True)
    own = everything[:, :COLS]
    up = [(i, i + 1) for i in range(slabs - 1)]
    before = lax.ppermute(own, "slab", up)
    after = lax.ppermute(own, "slab", [(j, i) for i, j in up])
    tid, geo, pos, info = call(
        list_kernel,
        (
            sds((SLOTS, BLK), F32),
            sds((13, SLOTS, BLK), F32),
            sds((6, SLOTS, BLK), jnp.int32),
            sds((2, SLOTS + 1), jnp.int32),
        ),
        [VMEM],
        (VMEM, VMEM, VMEM, SMEM),
        [
            vm((11, SLOTS, BLK), F32),
            vm((8, BLK), jnp.int32),
            pltpu.SMEM((8, BLK), jnp.int32),
            pltpu.SemaphoreType.DMA((1,)),
        ],
        10_000_000,
        1_000_000,
    )(everything)
    got = shared(arrived.astype(BF16))
    return call(
        apply_kernel,
        sds((COLS, probe.shape[1]), F32),
        [SMEM] + [VMEM] * 4 + [ANY] * 3,
        VMEM,
        [
            vm((BLK, RANKS * BLK), BF16),
            vm((6 * SLOTS, RANKS * BLK), BF16),
            vm((6, SLOTS, BLK), F32),
            vm((BLK, BLK), F32),
            vm((3 * SUBS, COLS, probe.shape[1]), BF16),
            vm((BLK_DEV, COLS, BLK), F32),
            pltpu.SemaphoreType.DMA((3,)),
        ],
        1_000_000_000,
        3_000_000,
    )(info, got, tid, geo, pos, before, own, after)


def solution(mesh):
    placed = (
        P(("slab", "sub"), None),
        P(None, ("slab", "sub")),
        P(),
        P(),
        P(),
        P(),
        P(None, None, ("slab", "sub")),
        P(("slab", "sub")),
        P(None, None, ("slab", "sub")),
        P(("slab", "sub")),
        P(("slab", "sub")),
        P(None, ("slab", "sub")),
    )
    return jax.shard_map(
        local, mesh=mesh, in_specs=placed, out_specs=P(None, ("slab", "sub")), check_vma=False
    )
```

```python
import jax
import jax.numpy as jnp
from jax import lax
from jax.experimental import pallas as pl
from jax.experimental.pallas import tpu as pltpu
from jax.sharding import PartitionSpec as P

BLK = 128
CHUNKS = 16
RANKS = 16
FIELDS = 8
SLOTS = 32
TILES_SLAB = 64
TILE_DEV = 16
SUBS = 4
BLK_DEV = 4
COLS = 64
PAIRS = ((0, 0), (0, 1), (0, 2), (1, 1), (1, 2), (2, 2))
PAIR_OF = {(a, b): PAIRS.index((min(a, b), max(a, b))) for a in range(3) for b in range(3)}
NT = (((1,), (1,)), ((), ()))
VMEM = pl.BlockSpec(memory_space=pltpu.VMEM)
SMEM = pl.BlockSpec(memory_space=pltpu.SMEM)
F32 = jnp.float32
BF16 = jnp.bfloat16
HBM = pl.BlockSpec(memory_space=pltpu.HBM)
ANY = pl.BlockSpec(memory_space=pl.ANY)
ELEM_FIELDS = 16
META = COLS + 4 * ELEM_FIELDS
SEND_ROWS = META + 16
UNROLL = 4


def call(kernel, out_shape, in_specs, out_specs, scratch, flops, nbytes, vmem=40):
    return pl.pallas_call(
        kernel,
        out_shape=out_shape,
        in_specs=in_specs,
        out_specs=out_specs,
        scratch_shapes=scratch,
        compiler_params=pltpu.CompilerParams(vmem_limit_bytes=vmem * 1024 * 1024),
        cost_estimate=pl.CostEstimate(flops=flops, bytes_accessed=nbytes, transcendentals=0),
    )


def lanes(chunk):
    return slice(chunk * BLK, (chunk + 1) * BLK)


def halves(x):
    high = x.astype(BF16)
    return high, (x - high.astype(F32)).astype(BF16)


def start_all(pairs, sem):
    copies = [pltpu.make_async_copy(s, d, sem.at[i]) for i, (s, d) in enumerate(pairs)]
    for c in copies:
        c.start()
    return copies


def pack_kernel(grad_hbm, area_hbm, corner_hbm, rows_ref, cols_ref, probe_hbm, send_ref, grad_ref, area_ref, corner_ref, meta_ref, sem):
    copies = start_all(
        ((grad_hbm, grad_ref), (area_hbm, area_ref), (corner_hbm, corner_ref), (probe_hbm, send_ref.at[0:COLS])), sem
    )
    meta_ref[...] = jnp.zeros(meta_ref.shape, F32)
    for i, ref in enumerate((rows_ref, cols_ref)):
        meta_ref[2 * i : 2 * i + 1, 0:TILE_DEV] = (ref[...] >> 4).astype(F32)
        meta_ref[2 * i + 1 : 2 * i + 2, 0:TILE_DEV] = (ref[...] & 15).astype(F32)
    send_ref[META:, :] = meta_ref[...].astype(BF16)
    for c in copies:
        c.wait()
    for q in range(4):
        here = slice(q * 512, (q + 1) * 512)
        values = [grad_ref[i, j : j + 1, here] for i in range(2) for j in range(2)] + [area_ref[:, here]]
        fields = [half.astype(F32) for v in values for half in halves(v)]
        fields += [corner_ref[a, side : side + 1, here].astype(F32) for side in range(2) for a in range(3)]
        top = COLS + q * ELEM_FIELDS
        send_ref[top : top + ELEM_FIELDS, :] = jnp.concatenate(fields, axis=0).astype(BF16)


def route_kernel(
    cov_hbm, slot_hbm, w1_hbm, b1_hbm, w2_hbm, b2_ref,
    out_ref,
    cov_ref, slot_ref, w1_ref, b1_ref, w2_ref, hot_ref, rank_ref, val_ref, par_ref, sem,
):
    copies = start_all(
        ((slot_hbm, slot_ref), (w1_hbm, w1_ref), (b1_hbm, b1_ref), (w2_hbm, w2_ref), (cov_hbm, cov_ref)), sem
    )
    slab_iota = lax.broadcasted_iota(jnp.int32, (BLK, BLK), 0)
    lane_iota = lax.broadcasted_iota(jnp.int32, (BLK, BLK), 1)
    earlier = jnp.concatenate(
        [jnp.where(slab_iota < lane_iota, 1.0, 0.0).astype(BF16), jnp.ones((BLK, BLK), BF16)], axis=1
    )
    copies[0].wait()
    for chunk in range(CHUNKS):
        slab = slot_ref[0:1, lanes(chunk)] >> 2
        hot_ref[:, lanes(chunk)] = jnp.where(slab_iota == slab, 1.0, 0.0).astype(BF16)
    seen = jnp.zeros((BLK, BLK), F32)
    for chunk in range(CHUNKS):
        hot = hot_ref[:, lanes(chunk)]
        counts = jnp.dot(hot, earlier, preferred_element_type=F32)
        rank_ref[:, lanes(chunk)] = jnp.sum(
            hot.astype(F32) * (counts[:, :BLK] + seen), axis=0, keepdims=True
        )
        seen = seen + counts[:, BLK:]
    for c in copies[1:]:
        c.wait()
    rows = 256
    for part in range(cov_ref.shape[0] // rows):
        here = slice(part * rows, (part + 1) * rows)
        pre_act = jnp.dot(cov_ref[here, :], w1_ref[...], preferred_element_type=F32) + b1_ref[...]
        hidden = jax.nn.gelu(pre_act, approximate=True).astype(BF16)
        par_ref[:, here] = lax.dot_general(w2_ref[...], hidden, NT, preferred_element_type=F32)
    rank_iota = lax.broadcasted_iota(jnp.int32, (RANKS, BLK), 0).astype(F32)
    for chunk in range(CHUNKS):
        device = slot_ref[0:1, lanes(chunk)]
        place = slot_ref[1:2, lanes(chunk)]
        values = []
        for f in range(3):
            values += [half.astype(F32) for half in halves(par_ref[f : f + 1, lanes(chunk)] + b2_ref[f])]
        values += [((device & 3) * TILE_DEV + (place >> 7)).astype(F32), (place & 127).astype(F32)]
        mine = rank_iota == rank_ref[:, lanes(chunk)]
        val_ref[:, lanes(chunk)] = jnp.concatenate(
            [jnp.where(mine, v, 0.0).astype(BF16) for v in values], axis=0
        )
    out_ref[...] = lax.dot_general(hot_ref[...], val_ref[...], NT, preferred_element_type=F32)


def list_kernel(
    s0_hbm, s1_hbm, s2_hbm, s3_hbm,
    tid_ref, geo_ref, pos_ref, info_ref,
    all_ref, raw_ref, ints_ref, meta_ref, sem, meta_sem,
):
    me = lax.axis_index("sub")
    base = (lax.axis_index("slab") - 1) * (SUBS * BLK_DEV)
    copies = start_all([(s, all_ref.at[i]) for i, s in enumerate((s0_hbm, s1_hbm, s2_hbm, s3_hbm))], sem)
    tid_ref[...] = jnp.full(tid_ref.shape, -1.0, F32)
    raw_ref[...] = jnp.zeros(raw_ref.shape, F32)
    for n in range(SLOTS):
        info_ref[0, n] = 0
        info_ref[1, n] = SUBS * BLK_DEV
    for c in copies:
        c.wait()
    for v in range(SUBS):
        coded = all_ref[v, META : META + 16, 0:BLK].astype(F32)
        for i in range(2):
            whole = coded[2 * i : 2 * i + 1] * 16.0 + coded[2 * i + 1 : 2 * i + 2]
            ints_ref[4 * i + v : 4 * i + v + 1, :] = whole.astype(jnp.int32)
    copy = pltpu.make_async_copy(ints_ref, meta_ref, meta_sem.at[0])
    copy.start()
    copy.wait()

    def find(t, n):
        v, k = t // TILE_DEV, t % TILE_DEV
        row = meta_ref[v, k]
        owned = (row // BLK_DEV) % SUBS == me

        @pl.when(owned)
        def _():
            tile = (me - v) % SUBS * TILE_DEV + k
            col = meta_ref[4 + v, k] - base
            step, s, blk = col // (SUBS * BLK_DEV), col // BLK_DEV % SUBS, col % BLK_DEV
            info_ref[0, n] = row % BLK_DEV
            info_ref[1, n] = (step * SUBS + (me - s) % SUBS) * BLK_DEV + blk
            tid_ref[pl.ds(n, 1), :] = jnp.full((1, BLK), tile, jnp.int32).astype(F32)
            top = pl.ds(pl.multiple_of(COLS + (k // 4) * ELEM_FIELDS, 16), ELEM_FIELDS)
            here = pl.ds(pl.multiple_of((k % 4) * BLK, BLK), BLK)
            raw_ref[pl.ds(n, 1)] = all_ref[v, top, here].astype(F32)[None]

        return n + owned.astype(jnp.int32)

    info_ref[0, SLOTS] = lax.fori_loop(0, TILES_SLAB, find, jnp.int32(0))
    field = [raw_ref[:, f, :] for f in range(ELEM_FIELDS)]
    value = [field[2 * i] + field[2 * i + 1] for i in range(5)]
    grad_x = [value[0], value[1], -(value[0] + value[1])]
    grad_y = [value[2], value[3], -(value[2] + value[3])]
    for i, (a, b) in enumerate(PAIRS):
        geo_ref[i] = grad_x[a] * grad_x[b] + grad_y[a] * grad_y[b]
        geo_ref[6 + i] = grad_x[a] * grad_y[b] + grad_y[a] * grad_x[b]
    geo_ref[12] = value[4]
    for a in range(6):
        pos_ref[a] = field[10 + a].astype(jnp.int32)


def matrix_kernel(got_ref, tid_ref, geo_ref, k_ref, hot_ref, val_ref, turned_ref):
    lane_iota = lax.broadcasted_iota(jnp.int32, (BLK, BLK), 0).astype(F32).astype(BF16)
    one, zero = jnp.ones((), BF16), jnp.zeros((), BF16)
    tiles = tid_ref[...].astype(BF16)
    found = jnp.zeros((6 * SLOTS, BLK), F32)
    for u in range(SUBS):
        turned_ref[...] = got_ref[u].astype(F32).T
        for k in range(RANKS):
            rows = [
                jnp.broadcast_to(turned_ref[f * RANKS + k : f * RANKS + k + 1, :], (16, BLK)).astype(BF16)
                for f in range(FIELDS)
            ]
            twice = [jnp.concatenate([r, r], axis=0) for r in rows[:7]]
            mine = tiles == twice[6]
            val_ref[:, lanes(k)] = jnp.concatenate([jnp.where(mine, twice[f], zero) for f in range(6)], axis=0)
            hot_ref[:, lanes(k)] = jnp.where(lane_iota == jnp.concatenate([rows[7]] * 8, axis=0), one, zero)
        found = found + lax.dot_general(val_ref[...], hot_ref[...], NT, preferred_element_type=F32)
    params = [
        found[2 * f * SLOTS : (2 * f + 1) * SLOTS] + found[(2 * f + 1) * SLOTS : (2 * f + 2) * SLOTS]
        for f in range(3)
    ]
    kappa_sq = jnp.exp(params[0])
    scale = jnp.exp(params[1])
    coupling = 0.9 * jnp.tanh(params[2])
    area = geo_ref[12]
    for i, (a, b) in enumerate(PAIRS):
        mass = kappa_sq * (2.0 if a == b else 1.0)
        stiffness = scale * (geo_ref[i] + coupling * geo_ref[6 + i])
        k_ref[i] = (area * (stiffness + mass)).astype(BF16).astype(F32)


def apply_kernel(
    info_ref, k_ref, pos_ref, before_hbm, own_hbm, after_hbm,
    out_ref, x_ref, acc_ref, sem,
):
    copies = start_all(
        [(src, x_ref.at[SUBS * i : SUBS * (i + 1)]) for i, src in enumerate((before_hbm, own_hbm, after_hbm))], sem
    )
    lane_iota = lax.broadcasted_iota(jnp.int32, (BLK, BLK), 0).astype(F32).astype(BF16)
    one, zero = jnp.ones((), BF16), jnp.zeros((), BF16)
    acc_ref[...] = jnp.zeros(acc_ref.shape, F32)
    for c in copies:
        c.wait()

    def tile_part(n):
        col = info_ref[1, n]
        where = pl.ds(pl.multiple_of((col % BLK_DEV) * BLK, BLK), BLK)
        x = x_ref[col // BLK_DEV, :, where].astype(F32)
        k = [k_ref[i, pl.ds(n, 1), :] for i in range(6)]
        xs = [
            jnp.take_along_axis(x, jnp.broadcast_to(pos_ref[3 + b, pl.ds(n, 1), :], (COLS, BLK)), axis=1)
            for b in range(3)
        ]
        ys = []
        hots = []
        for a in range(3):
            y = k[PAIR_OF[a, 0]] * xs[0] + k[PAIR_OF[a, 1]] * xs[1] + k[PAIR_OF[a, 2]] * xs[2]
            ys.append(y.astype(BF16))
            row = jnp.broadcast_to(pos_ref[a, pl.ds(n, 1), :].astype(F32), (16, BLK)).astype(BF16)
            hots.append(jnp.where(lane_iota == jnp.concatenate([row] * 8, axis=0), one, zero))
        return lax.dot_general(
            jnp.concatenate(ys, axis=1), jnp.concatenate(hots, axis=1), NT, preferred_element_type=F32
        )

    def add(group, carry):
        done = [tile_part(group * UNROLL + i) for i in range(UNROLL)]
        for i in range(UNROLL):
            block = info_ref[0, group * UNROLL + i]
            acc_ref[block] = acc_ref[block] + done[i]
        return carry

    lax.fori_loop(0, (info_ref[0, SLOTS] + UNROLL - 1) // UNROLL, add, jnp.int32(0))
    for block in range(BLK_DEV):
        out_ref[:, lanes(block)] = acc_ref[block]


def shared(block):
    copies = jnp.broadcast_to(block[None], (SUBS, *block.shape))
    return lax.all_to_all(copies, "sub", split_axis=0, concat_axis=0, tiled=True)


def route(covariates, partition_slot, in_weight, in_bias, out_weight, out_bias):
    elements = partition_slot.shape[1]
    vm = pltpu.VMEM
    return call(
        route_kernel,
        jax.ShapeDtypeStruct((BLK, BLK), F32),
        [HBM] * 5 + [SMEM],
        VMEM,
        [
            vm(covariates.shape, BF16),
            vm(partition_slot.shape, jnp.int32),
            vm(in_weight.shape, BF16),
            vm((1, in_bias.shape[0]), F32),
            vm(out_weight.shape, BF16),
            vm((BLK, elements), BF16),
            vm((1, elements), F32),
            vm((BLK, elements), BF16),
            vm((3, elements), F32),
            pltpu.SemaphoreType.DMA((5,)),
        ],
        400_000_000,
        1_000_000,
        60,
    )(covariates, partition_slot, in_weight, in_bias[None], out_weight, out_bias)


def pack(gradients, areas, corners, tile_rows, tile_cols, probe):
    vm = pltpu.VMEM
    return call(
        pack_kernel,
        jax.ShapeDtypeStruct((SEND_ROWS, probe.shape[1]), BF16),
        [HBM] * 3 + [VMEM] * 2 + [HBM],
        VMEM,
        [
            vm(gradients.shape, F32),
            vm((1, areas.shape[0]), F32),
            vm((3, 2, areas.shape[0]), jnp.int32),
            vm((16, probe.shape[1]), F32),
            pltpu.SemaphoreType.DMA((4,)),
        ],
        1_000_000,
        1_000_000,
        60,
    )(gradients, areas[None], corners.transpose(1, 0, 2), tile_rows[None], tile_cols[None], probe)


def listed(sends):
    sds = jax.ShapeDtypeStruct
    vm = pltpu.VMEM
    return call(
        list_kernel,
        (
            sds((SLOTS, BLK), F32),
            sds((13, SLOTS, BLK), F32),
            sds((6, SLOTS, BLK), jnp.int32),
            sds((2, SLOTS + 1), jnp.int32),
        ),
        [ANY] * 4,
        (VMEM, VMEM, VMEM, SMEM),
        [
            vm((SUBS, *sends[0].shape), BF16),
            vm((SLOTS, ELEM_FIELDS, BLK), F32),
            vm((8, BLK), jnp.int32),
            pltpu.SMEM((8, BLK), jnp.int32),
            pltpu.SemaphoreType.DMA((4,)),
            pltpu.SemaphoreType.DMA((1,)),
        ],
        10_000_000,
        1_000_000,
    )(*sends)


def matrices(got, tid, geo):
    vm = pltpu.VMEM
    return call(
        matrix_kernel,
        jax.ShapeDtypeStruct((6, SLOTS, BLK), F32),
        [VMEM] * 3,
        VMEM,
        [
            vm((BLK, RANKS * BLK), BF16),
            vm((6 * SLOTS, RANKS * BLK), BF16),
            vm((BLK, BLK), F32),
        ],
        1_000_000_000,
        3_000_000,
    )(got, tid, geo)


def applied(info, k, pos, before, own, after):
    vm = pltpu.VMEM
    return call(
        apply_kernel,
        jax.ShapeDtypeStruct((COLS, own.shape[2]), F32),
        [SMEM] + [VMEM] * 2 + [ANY] * 3,
        VMEM,
        [
            vm((3 * SUBS, *own.shape[1:]), BF16),
            vm((BLK_DEV, COLS, BLK), F32),
            pltpu.SemaphoreType.DMA((3,)),
        ],
        1_000_000_000,
        3_000_000,
    )(info, k, pos, before, own, after)


def local(
    covariates,
    partition_slot,
    in_weight,
    in_bias,
    out_weight,
    out_bias,
    gradients,
    areas,
    corners,
    tile_rows,
    tile_cols,
    probe,
):
    slabs = lax.axis_size("slab")
    routed = route(covariates, partition_slot, in_weight, in_bias, out_weight, out_bias)
    arrived = lax.all_to_all(routed, "slab", split_axis=0, concat_axis=0, tiled=True)
    send = pack(gradients, areas, corners, tile_rows, tile_cols, probe)
    sends = [send] + [lax.ppermute(send, "sub", [(i, (i + k) % SUBS) for i in range(SUBS)]) for k in (1, 2, 3)]
    got = shared(arrived.astype(BF16))
    own = jnp.stack([s[:COLS] for s in sends])
    up = [(i, i + 1) for i in range(slabs - 1)]
    before = lax.ppermute(own, "slab", up)
    after = lax.ppermute(own, "slab", [(j, i) for i, j in up])
    tid, geo, pos, info = listed(sends)
    return applied(info, matrices(got, tid, geo), pos, before, own, after)


def solution(mesh):
    placed = (
        P(("slab", "sub"), None),
        P(None, ("slab", "sub")),
        P(),
        P(),
        P(),
        P(),
        P(None, None, ("slab", "sub")),
        P(("slab", "sub")),
        P(None, None, ("slab", "sub")),
        P(("slab", "sub")),
        P(("slab", "sub")),
        P(None, ("slab", "sub")),
    )
    return jax.shard_map(
        local, mesh=mesh, in_specs=placed, out_specs=P(None, ("slab", "sub")), check_vma=False
    )
```

```python
import jax
import jax.numpy as jnp
from jax import lax
from jax.experimental import pallas as pl
from jax.experimental.pallas import tpu as pltpu
from jax.sharding import PartitionSpec as P

BLK = 128
CHUNKS = 16
RANKS = 16
FIELDS = 8
SLOTS = 32
TILES_SLAB = 64
TILE_DEV = 16
SUBS = 4
BLK_DEV = 4
COLS = 64
PAIRS = ((0, 0), (0, 1), (0, 2), (1, 1), (1, 2), (2, 2))
PAIR_OF = {(a, b): PAIRS.index((min(a, b), max(a, b))) for a in range(3) for b in range(3)}
NT = (((1,), (1,)), ((), ()))
VMEM = pl.BlockSpec(memory_space=pltpu.VMEM)
SMEM = pl.BlockSpec(memory_space=pltpu.SMEM)
F32 = jnp.float32
BF16 = jnp.bfloat16
HBM = pl.BlockSpec(memory_space=pltpu.HBM)
ANY = pl.BlockSpec(memory_space=pl.ANY)
ELEM_FIELDS = 16
ROUTED = 32
ELEMS = ROUTED + COLS
META = ELEMS + 4 * TILE_DEV
SEND_ROWS = META + 16
UNROLL = 4


def call(kernel, out_shape, in_specs, out_specs, scratch, flops, nbytes, vmem=40):
    return pl.pallas_call(
        kernel,
        out_shape=out_shape,
        in_specs=in_specs,
        out_specs=out_specs,
        scratch_shapes=scratch,
        compiler_params=pltpu.CompilerParams(vmem_limit_bytes=vmem * 1024 * 1024),
        cost_estimate=pl.CostEstimate(flops=flops, bytes_accessed=nbytes, transcendentals=0),
    )


def lanes(chunk):
    return slice(chunk * BLK, (chunk + 1) * BLK)


def halves(x):
    high = x.astype(BF16)
    return high, (x - high.astype(F32)).astype(BF16)


def start_all(pairs, sem):
    copies = [pltpu.make_async_copy(s, d, sem.at[i]) for i, (s, d) in enumerate(pairs)]
    for c in copies:
        c.start()
    return copies


def front_kernel(
    cov_hbm, slot_hbm, w1_hbm, b1_hbm, w2_hbm, b2_ref, grad_hbm, area_hbm, corner_hbm, rows_ref, cols_ref, probe_hbm,
    out_hbm,
    cov_ref, slot_ref, w1_ref, b1_ref, w2_ref, grad_ref, area_ref, corner_ref, meta_ref,
    hot_ref, rank_ref, val_ref, par_ref, send_ref, sem, out_sem,
):
    copies = start_all(
        (
            (slot_hbm, slot_ref), (grad_hbm, grad_ref), (area_hbm, area_ref), (corner_hbm, corner_ref),
            (probe_hbm, send_ref.at[ROUTED:ELEMS]),
            (w1_hbm, w1_ref), (b1_hbm, b1_ref), (w2_hbm, w2_ref), (cov_hbm, cov_ref),
        ),
        sem,
    )
    meta_ref[...] = jnp.zeros(meta_ref.shape, F32)
    for i, ref in enumerate((rows_ref, cols_ref)):
        meta_ref[2 * i : 2 * i + 1, 0:TILE_DEV] = (ref[...] >> 4).astype(F32)
        meta_ref[2 * i + 1 : 2 * i + 2, 0:TILE_DEV] = (ref[...] & 15).astype(F32)
    meta = pltpu.roll(meta_ref[...], lax.axis_index("sub") * TILE_DEV, 1).astype(BF16)
    send_ref[META:, :] = jnp.concatenate([meta, jnp.zeros((16, 3 * BLK), BF16)], axis=1)
    slab_iota = lax.broadcasted_iota(jnp.int32, (BLK, BLK), 0)
    lane_iota = lax.broadcasted_iota(jnp.int32, (BLK, BLK), 1)
    earlier = jnp.concatenate(
        [jnp.where(slab_iota < lane_iota, 1.0, 0.0).astype(BF16), jnp.ones((BLK, BLK), BF16)], axis=1
    )
    copies[0].wait()
    for chunk in range(CHUNKS):
        slab = slot_ref[0:1, lanes(chunk)] >> 2
        hot_ref[:, lanes(chunk)] = jnp.where(slab_iota == slab, 1.0, 0.0).astype(BF16)
    seen = jnp.zeros((BLK, BLK), F32)
    for chunk in range(CHUNKS):
        hot = hot_ref[:, lanes(chunk)]
        counts = jnp.dot(hot, earlier, preferred_element_type=F32)
        rank_ref[:, lanes(chunk)] = jnp.sum(
            hot.astype(F32) * (counts[:, :BLK] + seen), axis=0, keepdims=True
        )
        seen = seen + counts[:, BLK:]
    for c in copies[1:5]:
        c.wait()
    for group in range(4):
        for f in range(4):
            field = 4 * group + f
            if field < 10:
                v = field // 2
                row = area_ref[...] if v == 4 else grad_ref[v // 2, v % 2 : v % 2 + 1, :]
                part = halves(row)[field % 2].astype(F32)
            else:
                a, side = (field - 10) % 3, (field - 10) // 3
                part = corner_ref[a, side : side + 1, :].astype(F32)
            top = ELEMS + group * TILE_DEV
            send_ref[top : top + TILE_DEV, lanes(f)] = jnp.concatenate(
                [part[:, lanes(k)] for k in range(TILE_DEV)], axis=0
            ).astype(BF16)
    outs = start_all([(send_ref.at[ROUTED:], out_hbm.at[i, ROUTED:]) for i in range(SUBS)], out_sem)
    for c in copies[5:]:
        c.wait()
    rows = 256
    for part in range(cov_ref.shape[0] // rows):
        here = slice(part * rows, (part + 1) * rows)
        pre_act = jnp.dot(cov_ref[here, :], w1_ref[...], preferred_element_type=F32) + b1_ref[...]
        hidden = jax.nn.gelu(pre_act, approximate=True).astype(BF16)
        par_ref[:, here] = lax.dot_general(w2_ref[...], hidden, NT, preferred_element_type=F32)
    rank_iota = lax.broadcasted_iota(jnp.int32, (RANKS, BLK), 0).astype(F32)
    for chunk in range(CHUNKS):
        device = slot_ref[0:1, lanes(chunk)]
        place = slot_ref[1:2, lanes(chunk)]
        values = []
        for f in range(3):
            values += [half.astype(F32) for half in halves(par_ref[f : f + 1, lanes(chunk)] + b2_ref[f])]
        values += [((device & 3) * TILE_DEV + (place >> 7)).astype(F32), (place & 127).astype(F32)]
        mine = rank_iota == rank_ref[:, lanes(chunk)]
        val_ref[:, lanes(chunk)] = jnp.concatenate(
            [jnp.where(mine, v, 0.0).astype(BF16) for v in values], axis=0
        )
    routed = lax.dot_general(hot_ref[...], val_ref[...], NT, preferred_element_type=F32).astype(BF16)
    for j in range(4):
        send_ref[0:ROUTED, lanes(j)] = routed[j * ROUTED : (j + 1) * ROUTED]
    outs += [pltpu.make_async_copy(send_ref.at[:ROUTED], out_hbm.at[i, :ROUTED], out_sem.at[SUBS + i]) for i in range(SUBS)]
    for c in outs[SUBS:]:
        c.start()
    for c in outs:
        c.wait()


def list_kernel(all_ref, tid_ref, geo_ref, pos_ref, info_ref):
    me = lax.axis_index("sub")
    base = (lax.axis_index("slab") - 1) * (SUBS * BLK_DEV)
    coded = all_ref[0, META:, 0:BLK].astype(F32)
    for u in range(1, SUBS):
        coded = coded + all_ref[u, META:, 0:BLK].astype(F32)
    row = (coded[0:1] * 16.0 + coded[1:2]).astype(jnp.int32)
    col = (coded[2:3] * 16.0 + coded[3:4]).astype(jnp.int32) - base
    tile = lax.broadcasted_iota(jnp.int32, (1, BLK), 1)
    mine = (((row >> 2) & 3) == me) & (tile < TILES_SLAB)
    mine = jnp.where(mine, 1.0, 0.0)
    earlier = jnp.where(
        lax.broadcasted_iota(jnp.int32, (BLK, BLK), 0) < lax.broadcasted_iota(jnp.int32, (BLK, BLK), 1), 1.0, 0.0
    )
    rank = jnp.dot(
        jnp.broadcast_to(mine, (16, BLK)).astype(BF16), earlier.astype(BF16), preferred_element_type=F32
    )[0:1]
    slot_iota = lax.broadcasted_iota(jnp.int32, (SLOTS, BLK), 0).astype(F32)
    pick = jnp.where((slot_iota == rank) & (mine > 0.0), 1.0, 0.0)
    tiles = jnp.sum(pick * tile.astype(F32), axis=1, keepdims=True)
    used = jnp.sum(pick, axis=1, keepdims=True)
    tid_ref[...] = jnp.broadcast_to(jnp.where(used > 0.0, tiles, -1.0), (SLOTS, BLK))
    count = jnp.broadcast_to(jnp.sum(mine, axis=1, keepdims=True), (1, BLK))
    pick = pick.astype(BF16)
    facts = jnp.concatenate(
        [(row & 3).astype(F32), jnp.clip(col, 0, 47).astype(F32), jnp.zeros((14, BLK), F32)], axis=0
    ).astype(BF16)
    wide = jnp.concatenate([pick, jnp.zeros((BLK - SLOTS, BLK), BF16)], axis=0)
    facts = lax.dot_general(facts, wide, NT, preferred_element_type=F32)
    info_ref[...] = jnp.concatenate([facts[0:2], count, jnp.zeros((5, BLK), F32)], axis=0).astype(jnp.int32)
    field = []
    for group in range(4):
        here = slice(ELEMS + group * TILE_DEV, ELEMS + (group + 1) * TILE_DEV)
        stacked = jnp.concatenate([all_ref[u, here, :] for u in range(SUBS)], axis=0)
        got = jnp.dot(pick[:, :TILES_SLAB], stacked, preferred_element_type=F32)
        field += [got[:, lanes(f)] for f in range(4)]
    value = [field[2 * i] + field[2 * i + 1] for i in range(5)]
    grad_x = [value[0], value[1], -(value[0] + value[1])]
    grad_y = [value[2], value[3], -(value[2] + value[3])]
    for i, (a, b) in enumerate(PAIRS):
        geo_ref[i] = grad_x[a] * grad_x[b] + grad_y[a] * grad_y[b]
        geo_ref[6 + i] = grad_x[a] * grad_y[b] + grad_y[a] * grad_x[b]
    geo_ref[12] = value[4]
    for a in range(6):
        pos_ref[a] = field[10 + a].astype(jnp.int32)


def matrix_kernel(got_ref, tid_ref, geo_ref, k_ref, hot_ref, val_ref, turned_ref):
    lane_iota = lax.broadcasted_iota(jnp.int32, (BLK, BLK), 0).astype(F32).astype(BF16)
    one, zero = jnp.ones((), BF16), jnp.zeros((), BF16)
    tiles = tid_ref[...].astype(BF16)
    found = jnp.zeros((6 * SLOTS, BLK), F32)
    for u in range(SUBS):
        turned_ref[...] = got_ref[lanes(u), :].astype(F32).T
        for k in range(RANKS):
            rows = [
                jnp.broadcast_to(turned_ref[f * RANKS + k : f * RANKS + k + 1, :], (16, BLK)).astype(BF16)
                for f in range(FIELDS)
            ]
            twice = [jnp.concatenate([r, r], axis=0) for r in rows[:7]]
            mine = tiles == twice[6]
            val_ref[:, lanes(k)] = jnp.concatenate([jnp.where(mine, twice[f], zero) for f in range(6)], axis=0)
            hot_ref[:, lanes(k)] = jnp.where(lane_iota == jnp.concatenate([rows[7]] * 8, axis=0), one, zero)
        found = found + lax.dot_general(val_ref[...], hot_ref[...], NT, preferred_element_type=F32)
    params = [
        found[2 * f * SLOTS : (2 * f + 1) * SLOTS] + found[(2 * f + 1) * SLOTS : (2 * f + 2) * SLOTS]
        for f in range(3)
    ]
    kappa_sq = jnp.exp(params[0])
    scale = jnp.exp(params[1])
    coupling = 0.9 * jnp.tanh(params[2])
    area = geo_ref[12]
    for i, (a, b) in enumerate(PAIRS):
        mass = kappa_sq * (2.0 if a == b else 1.0)
        stiffness = scale * (geo_ref[i] + coupling * geo_ref[6 + i])
        k_ref[i] = (area * (stiffness + mass)).astype(BF16).astype(F32)


def apply_kernel(
    info_ref, k_ref, pos_ref, before_hbm, own_hbm, after_hbm,
    out_ref, x_ref, acc_ref, sem,
):
    copies = start_all(
        [(src, x_ref.at[SUBS * i : SUBS * (i + 1)]) for i, src in enumerate((before_hbm, own_hbm, after_hbm))], sem
    )
    lane_iota = lax.broadcasted_iota(jnp.int32, (BLK, BLK), 0).astype(F32).astype(BF16)
    one, zero = jnp.ones((), BF16), jnp.zeros((), BF16)
    acc_ref[...] = jnp.zeros(acc_ref.shape, F32)
    for c in copies:
        c.wait()

    def tile_part(n):
        col = info_ref[1, n]
        where = pl.ds(pl.multiple_of((col % BLK_DEV) * BLK, BLK), BLK)
        x = x_ref[col // BLK_DEV, :, where].astype(F32)
        k = [k_ref[i, pl.ds(n, 1), :] for i in range(6)]
        xs = [
            jnp.take_along_axis(x, jnp.broadcast_to(pos_ref[3 + b, pl.ds(n, 1), :], (COLS, BLK)), axis=1)
            for b in range(3)
        ]
        ys = []
        hots = []
        for a in range(3):
            y = k[PAIR_OF[a, 0]] * xs[0] + k[PAIR_OF[a, 1]] * xs[1] + k[PAIR_OF[a, 2]] * xs[2]
            ys.append(y.astype(BF16))
            row = jnp.broadcast_to(pos_ref[a, pl.ds(n, 1), :].astype(F32), (16, BLK)).astype(BF16)
            hots.append(jnp.where(lane_iota == jnp.concatenate([row] * 8, axis=0), one, zero))
        return lax.dot_general(
            jnp.concatenate(ys, axis=1), jnp.concatenate(hots, axis=1), NT, preferred_element_type=F32
        )

    def add(group, carry):
        done = [tile_part(group * UNROLL + i) for i in range(UNROLL)]
        for i in range(UNROLL):
            block = info_ref[0, group * UNROLL + i]
            acc_ref[block] = acc_ref[block] + done[i]
        return carry

    lax.fori_loop(0, (info_ref[2, 0] + UNROLL - 1) // UNROLL, add, jnp.int32(0))
    for block in range(BLK_DEV):
        out_ref[:, lanes(block)] = acc_ref[block]


def front(covariates, partition_slot, in_weight, in_bias, out_weight, out_bias, gradients, areas, corners, tile_rows, tile_cols, probe):
    elements = areas.shape[0]
    vm = pltpu.VMEM
    return call(
        front_kernel,
        jax.ShapeDtypeStruct((SUBS, SEND_ROWS, probe.shape[1]), BF16),
        [HBM] * 5 + [SMEM] + [HBM] * 3 + [VMEM] * 2 + [HBM],
        HBM,
        [
            vm(covariates.shape, BF16),
            vm(partition_slot.shape, jnp.int32),
            vm(in_weight.shape, BF16),
            vm((1, in_bias.shape[0]), F32),
            vm(out_weight.shape, BF16),
            vm(gradients.shape, F32),
            vm((1, elements), F32),
            vm((3, 2, elements), jnp.int32),
            vm((16, BLK), F32),
            vm((BLK, elements), BF16),
            vm((1, elements), F32),
            vm((BLK, elements), BF16),
            vm((3, elements), F32),
            vm((SEND_ROWS, probe.shape[1]), BF16),
            pltpu.SemaphoreType.DMA((9,)),
            pltpu.SemaphoreType.DMA((2 * SUBS,)),
        ],
        400_000_000,
        1_000_000,
        60,
    )(
        covariates, partition_slot, in_weight, in_bias[None], out_weight, out_bias,
        gradients, areas[None], corners.transpose(1, 0, 2), tile_rows[None], tile_cols[None], probe,
    )


def listed(everything):
    sds = jax.ShapeDtypeStruct
    return call(
        list_kernel,
        (
            sds((SLOTS, BLK), F32),
            sds((13, SLOTS, BLK), F32),
            sds((6, SLOTS, BLK), jnp.int32),
            sds((8, BLK), jnp.int32),
        ),
        [VMEM],
        (VMEM,) * 4,
        (),
        10_000_000,
        1_000_000,
    )(everything)


def matrices(got, tid, geo):
    vm = pltpu.VMEM
    return call(
        matrix_kernel,
        jax.ShapeDtypeStruct((6, SLOTS, BLK), F32),
        [VMEM] * 3,
        VMEM,
        [
            vm((BLK, RANKS * BLK), BF16),
            vm((6 * SLOTS, RANKS * BLK), BF16),
            vm((BLK, BLK), F32),
        ],
        1_000_000_000,
        3_000_000,
    )(got, tid, geo)


def applied(info, k, pos, before, own, after):
    vm = pltpu.VMEM
    return call(
        apply_kernel,
        jax.ShapeDtypeStruct((COLS, own.shape[2]), F32),
        [SMEM] + [VMEM] * 2 + [ANY] * 3,
        VMEM,
        [
            vm((3 * SUBS, *own.shape[1:]), BF16),
            vm((BLK_DEV, COLS, BLK), F32),
            pltpu.SemaphoreType.DMA((3,)),
        ],
        1_000_000_000,
        3_000_000,
    )(info, k, pos, before, own, after)


def local(
    covariates,
    partition_slot,
    in_weight,
    in_bias,
    out_weight,
    out_bias,
    gradients,
    areas,
    corners,
    tile_rows,
    tile_cols,
    probe,
):
    slabs = lax.axis_size("slab")
    send = front(
        covariates, partition_slot, in_weight, in_bias, out_weight, out_bias,
        gradients, areas, corners, tile_rows, tile_cols, probe,
    )
    everything = lax.all_to_all(send, "sub", split_axis=0, concat_axis=0, tiled=True)
    routed = everything[:, :ROUTED].reshape(SUBS, ROUTED, 4, BLK).transpose(2, 1, 0, 3)
    routed = routed.reshape(4 * ROUTED, SUBS, BLK)
    got = lax.all_to_all(routed, "slab", split_axis=0, concat_axis=0, tiled=True)
    own = everything[:, ROUTED:ELEMS]
    up = [(i, i + 1) for i in range(slabs - 1)]
    before = lax.ppermute(own, "slab", up)
    after = lax.ppermute(own, "slab", [(j, i) for i, j in up])
    tid, geo, pos, info = listed(everything)
    k = matrices(got.reshape(-1, BLK), tid, geo)
    return applied(info, k, pos, before, own, after)


def solution(mesh):
    placed = (
        P(("slab", "sub"), None),
        P(None, ("slab", "sub")),
        P(),
        P(),
        P(),
        P(),
        P(None, None, ("slab", "sub")),
        P(("slab", "sub")),
        P(None, None, ("slab", "sub")),
        P(("slab", "sub")),
        P(("slab", "sub")),
        P(None, ("slab", "sub")),
    )
    return jax.shard_map(
        local, mesh=mesh, in_specs=placed, out_specs=P(None, ("slab", "sub")), check_vma=False
    )
```

```python
import jax
import jax.numpy as jnp
from jax import lax
from jax.experimental import pallas as pl
from jax.experimental.pallas import tpu as pltpu
from jax.sharding import PartitionSpec as P

BLK = 128
CHUNKS = 16
RANKS = 16
FIELDS = 8
SLOTS = 32
TILE_DEV = 16
SUBS = 4
BLK_DEV = 4
COLS = 64
PAIRS = ((0, 0), (0, 1), (0, 2), (1, 1), (1, 2), (2, 2))
PAIR_OF = {(a, b): PAIRS.index((min(a, b), max(a, b))) for a in range(3) for b in range(3)}
NT = (((1,), (1,)), ((), ()))
VMEM = pl.BlockSpec(memory_space=pltpu.VMEM)
SMEM = pl.BlockSpec(memory_space=pltpu.SMEM)
F32 = jnp.float32
BF16 = jnp.bfloat16
HBM = pl.BlockSpec(memory_space=pltpu.HBM)
ANY = pl.BlockSpec(memory_space=pl.ANY)
OWNED = 8
ELEM_FIELDS = 18
PROBE = BLK
ELEMS = PROBE + BLK_DEV * COLS
SEND_ROWS = ELEMS + ELEM_FIELDS * OWNED
UNROLL = 4


def call(kernel, out_shape, in_specs, out_specs, scratch, flops, nbytes, vmem=40):
    return pl.pallas_call(
        kernel,
        out_shape=out_shape,
        in_specs=in_specs,
        out_specs=out_specs,
        scratch_shapes=scratch,
        compiler_params=pltpu.CompilerParams(vmem_limit_bytes=vmem * 1024 * 1024),
        cost_estimate=pl.CostEstimate(flops=flops, bytes_accessed=nbytes, transcendentals=0),
    )


def lanes(chunk):
    return slice(chunk * BLK, (chunk + 1) * BLK)


def halves(x):
    high = x.astype(BF16)
    return high, (x - high.astype(F32)).astype(BF16)


def start_all(pairs, sem):
    copies = [pltpu.make_async_copy(s, d, sem.at[i]) for i, (s, d) in enumerate(pairs)]
    for c in copies:
        c.start()
    return copies


def front_kernel(
    cov_hbm, slot_hbm, w1_hbm, b1_hbm, w2_hbm, b2_ref, grad_hbm, area_hbm, corner_hbm, rows_ref, cols_ref, probe_hbm,
    out_hbm,
    cov_ref, slot_ref, w1_ref, b1_ref, w2_ref, grad_ref, area_ref, corner_ref, tile_ref,
    hot_ref, rank_ref, val_ref, par_ref, send_ref, elem_ref, sem, out_sem,
):
    copies = start_all(
        (
            (slot_hbm, slot_ref), (grad_hbm, grad_ref), (area_hbm, area_ref), (corner_hbm, corner_ref),
            (w1_hbm, w1_ref), (b1_hbm, b1_ref), (w2_hbm, w2_ref), (cov_hbm, cov_ref),
            *(
                (probe_hbm.at[:, lanes(b)], send_ref.at[PROBE + b * COLS : PROBE + (b + 1) * COLS])
                for b in range(BLK_DEV)
            ),
        ),
        sem,
    )
    slab_iota = lax.broadcasted_iota(jnp.int32, (BLK, BLK), 0)
    lane_iota = lax.broadcasted_iota(jnp.int32, (BLK, BLK), 1)
    before = jnp.where(slab_iota < lane_iota, 1.0, 0.0).astype(BF16)
    earlier = jnp.concatenate([before, jnp.ones((BLK, BLK), BF16)], axis=1)
    tile_ref[...] = jnp.full(tile_ref.shape, -1.0, F32)
    tile_ref[0:1, 0:TILE_DEV] = rows_ref[...].astype(F32)
    tile_ref[1:2, 0:TILE_DEV] = cols_ref[...].astype(F32)
    row = tile_ref[0:1, :].astype(jnp.int32)
    col = tile_ref[1:2, :].astype(jnp.int32)
    real = lane_iota[0:1] < TILE_DEV
    owner = (row >> 2) & (SUBS - 1)
    mine = jnp.concatenate(
        [jnp.where(real & (owner == d), 1.0, 0.0) for d in range(SUBS)] + [jnp.zeros((12, BLK), F32)], axis=0
    )
    place = jnp.dot(mine.astype(BF16), before, preferred_element_type=F32)
    slot_iota = slab_iota[0:OWNED].astype(F32)
    pick = jnp.concatenate(
        [
            jnp.where((slot_iota == place[d : d + 1]) & (mine[d : d + 1] > 0.0), 1.0, 0.0)
            for d in range(SUBS)
        ],
        axis=0,
    ).astype(BF16)[:, :TILE_DEV]
    facts = [
        (lane_iota[0:1] + (lax.axis_index("sub") * TILE_DEV + 1)).astype(F32),
        (row & (BLK_DEV - 1)).astype(F32),
        (col >> 4).astype(F32),
        (col & 15).astype(F32),
    ]
    facts = jnp.concatenate([jnp.where(real, f, 0.0) for f in facts] + [jnp.zeros((BLK - 4, BLK), F32)], axis=0).T
    copies[0].wait()
    for chunk in range(CHUNKS):
        slab = slot_ref[0:1, lanes(chunk)] >> 2
        hot_ref[:, lanes(chunk)] = jnp.where(slab_iota == slab, 1.0, 0.0).astype(BF16)
    seen = jnp.zeros((BLK, BLK), F32)
    for chunk in range(CHUNKS):
        hot = hot_ref[:, lanes(chunk)]
        counts = jnp.dot(hot, earlier, preferred_element_type=F32)
        rank_ref[:, lanes(chunk)] = jnp.sum(
            hot.astype(F32) * (counts[:, :BLK] + seen), axis=0, keepdims=True
        )
        seen = seen + counts[:, BLK:]
    for c in copies[1:4]:
        c.wait()
    fields = []
    for v in range(5):
        value = area_ref[...] if v == 4 else grad_ref[v // 2, v % 2 : v % 2 + 1, :]
        fields += [half.astype(F32) for half in halves(value)]
    for side in range(2):
        for a in range(3):
            fields.append(corner_ref[a, side : side + 1, :].astype(F32))
    fields = [jnp.concatenate([f[:, lanes(k)] for k in range(TILE_DEV)], axis=0) for f in fields]
    fields += [facts[:TILE_DEV], jnp.zeros((TILE_DEV, BLK), F32)]
    picked = jnp.dot(pick, jnp.concatenate(fields, axis=1).astype(BF16), preferred_element_type=F32)
    for d in range(SUBS):
        elem_ref[d] = jnp.concatenate(
            [picked[d * OWNED : (d + 1) * OWNED, lanes(f)] for f in range(ELEM_FIELDS)], axis=0
        ).astype(BF16)
    for c in copies[8:]:
        c.wait()
    outs = start_all(
        [(send_ref.at[PROBE:], out_hbm.at[d, PROBE:ELEMS]) for d in range(SUBS)]
        + [(elem_ref.at[d], out_hbm.at[d, ELEMS:]) for d in range(SUBS)],
        out_sem,
    )
    for c in copies[4:8]:
        c.wait()
    rows = 256
    for part in range(cov_ref.shape[0] // rows):
        here = slice(part * rows, (part + 1) * rows)
        pre_act = jnp.dot(cov_ref[here, :], w1_ref[...], preferred_element_type=F32) + b1_ref[...]
        hidden = jax.nn.gelu(pre_act, approximate=True).astype(BF16)
        par_ref[:, here] = lax.dot_general(w2_ref[...], hidden, NT, preferred_element_type=F32)
    rank_iota = lax.broadcasted_iota(jnp.int32, (RANKS, BLK), 0).astype(F32)
    for chunk in range(CHUNKS):
        device = slot_ref[0:1, lanes(chunk)]
        place = slot_ref[1:2, lanes(chunk)]
        values = []
        for f in range(3):
            values += [half.astype(F32) for half in halves(par_ref[f : f + 1, lanes(chunk)] + b2_ref[f])]
        values += [((device & 3) * TILE_DEV + (place >> 7)).astype(F32), (place & 127).astype(F32)]
        ranked = rank_iota == rank_ref[:, lanes(chunk)]
        val_ref[:, lanes(chunk)] = jnp.concatenate(
            [jnp.where(ranked, v, 0.0).astype(BF16) for v in values], axis=0
        )
    send_ref[0:PROBE, :] = lax.dot_general(
        hot_ref[...], val_ref[...], NT, preferred_element_type=F32
    ).astype(BF16)
    last = [
        pltpu.make_async_copy(send_ref.at[:PROBE], out_hbm.at[d, :PROBE], out_sem.at[2 * SUBS + d])
        for d in range(SUBS)
    ]
    for c in last:
        c.start()
    for c in outs + last:
        c.wait()


def list_kernel(all_ref, tid_ref, geo_ref, pos_ref, info_ref):
    base = (lax.axis_index("slab") - 1) * (SUBS * BLK_DEV)
    sent = [all_ref[u, ELEMS:, :].astype(F32) for u in range(SUBS)]
    field = [
        jnp.concatenate([e[f * OWNED : (f + 1) * OWNED] for e in sent], axis=0) for f in range(ELEM_FIELDS - 1)
    ]
    facts = jnp.concatenate([field[16], jnp.zeros((BLK - SLOTS, BLK), F32)], axis=0)
    tid_ref[...] = jnp.broadcast_to(facts[:SLOTS, 0:1] - 1.0, (SLOTS, BLK))
    facts = facts.T
    col = (facts[2:3] * 16.0 + facts[3:4]).astype(jnp.int32) - base
    col = jnp.where(facts[0:1] > 0.0, col, SUBS * BLK_DEV)
    info_ref[...] = jnp.concatenate(
        [facts[1:2].astype(jnp.int32), col, jnp.zeros((6, BLK), jnp.int32)], axis=0
    )
    value = [field[2 * i] + field[2 * i + 1] for i in range(5)]
    grad_x = [value[0], value[1], -(value[0] + value[1])]
    grad_y = [value[2], value[3], -(value[2] + value[3])]
    for i, (a, b) in enumerate(PAIRS):
        geo_ref[i] = grad_x[a] * grad_x[b] + grad_y[a] * grad_y[b]
        geo_ref[6 + i] = grad_x[a] * grad_y[b] + grad_y[a] * grad_x[b]
    geo_ref[12] = value[4]
    for a in range(6):
        pos_ref[a] = field[10 + a].astype(jnp.int32)


def finish_kernel(
    info_ref, got_ref, tid_ref, geo_ref, pos_ref, before_hbm, own_hbm, after_hbm,
    out_ref, hot_ref, val_ref, turned_ref, k_ref, x_ref, acc_ref, sem,
):
    blocks = SUBS * BLK_DEV
    copies = start_all(
        [(src, x_ref.at[blocks * i : blocks * (i + 1)]) for i, src in enumerate((before_hbm, own_hbm, after_hbm))], sem
    )
    lane_iota = lax.broadcasted_iota(jnp.int32, (BLK, BLK), 0).astype(F32).astype(BF16)
    one, zero = jnp.ones((), BF16), jnp.zeros((), BF16)
    tiles = tid_ref[...].astype(BF16)
    found = jnp.zeros((6 * SLOTS, BLK), F32)
    for u in range(SUBS):
        turned_ref[...] = got_ref[lanes(u), :].astype(F32).T
        for k in range(RANKS):
            rows = [
                jnp.broadcast_to(turned_ref[f * RANKS + k : f * RANKS + k + 1, :], (16, BLK)).astype(BF16)
                for f in range(FIELDS)
            ]
            twice = [jnp.concatenate([r, r], axis=0) for r in rows[:7]]
            mine = tiles == twice[6]
            val_ref[:, lanes(k)] = jnp.concatenate([jnp.where(mine, twice[f], zero) for f in range(6)], axis=0)
            hot_ref[:, lanes(k)] = jnp.where(lane_iota == jnp.concatenate([rows[7]] * 8, axis=0), one, zero)
        found = found + lax.dot_general(val_ref[...], hot_ref[...], NT, preferred_element_type=F32)
    params = [
        found[2 * f * SLOTS : (2 * f + 1) * SLOTS] + found[(2 * f + 1) * SLOTS : (2 * f + 2) * SLOTS]
        for f in range(3)
    ]
    kappa_sq = jnp.exp(params[0])
    scale = jnp.exp(params[1])
    coupling = 0.9 * jnp.tanh(params[2])
    area = geo_ref[12]
    for i, (a, b) in enumerate(PAIRS):
        mass = kappa_sq * (2.0 if a == b else 1.0)
        stiffness = scale * (geo_ref[i] + coupling * geo_ref[6 + i])
        k_ref[i] = (area * (stiffness + mass)).astype(BF16).astype(F32)
    acc_ref[...] = jnp.zeros(acc_ref.shape, F32)
    for c in copies:
        c.wait()

    def tile_part(n):
        x = x_ref[info_ref[1, n]].astype(F32)
        k = [k_ref[i, pl.ds(n, 1), :] for i in range(6)]
        xs = [
            jnp.take_along_axis(x, jnp.broadcast_to(pos_ref[3 + b, pl.ds(n, 1), :], (COLS, BLK)), axis=1)
            for b in range(3)
        ]
        ys = []
        hots = []
        for a in range(3):
            y = k[PAIR_OF[a, 0]] * xs[0] + k[PAIR_OF[a, 1]] * xs[1] + k[PAIR_OF[a, 2]] * xs[2]
            ys.append(y.astype(BF16))
            row = jnp.broadcast_to(pos_ref[a, pl.ds(n, 1), :].astype(F32), (16, BLK)).astype(BF16)
            hots.append(jnp.where(lane_iota == jnp.concatenate([row] * 8, axis=0), one, zero))
        return lax.dot_general(
            jnp.concatenate(ys, axis=1), jnp.concatenate(hots, axis=1), NT, preferred_element_type=F32
        )

    def add(group, carry):
        done = [tile_part(group * UNROLL + i) for i in range(UNROLL)]
        for i in range(UNROLL):
            block = info_ref[0, group * UNROLL + i]
            acc_ref[block] = acc_ref[block] + done[i]
        return carry

    lax.fori_loop(0, SLOTS // UNROLL, add, jnp.int32(0))
    for block in range(BLK_DEV):
        out_ref[:, lanes(block)] = acc_ref[block]


def front(covariates, partition_slot, in_weight, in_bias, out_weight, out_bias, gradients, areas, corners, tile_rows, tile_cols, probe):
    elements = areas.shape[0]
    vm = pltpu.VMEM
    return call(
        front_kernel,
        jax.ShapeDtypeStruct((SUBS, SEND_ROWS, BLK), BF16),
        [HBM] * 5 + [SMEM] + [HBM] * 3 + [VMEM] * 2 + [HBM],
        HBM,
        [
            vm(covariates.shape, BF16),
            vm(partition_slot.shape, jnp.int32),
            vm(in_weight.shape, BF16),
            vm((1, in_bias.shape[0]), F32),
            vm(out_weight.shape, BF16),
            vm(gradients.shape, F32),
            vm((1, elements), F32),
            vm((3, 2, elements), jnp.int32),
            vm((8, BLK), F32),
            vm((BLK, elements), BF16),
            vm((1, elements), F32),
            vm((BLK, elements), BF16),
            vm((3, elements), F32),
            vm((ELEMS, BLK), BF16),
            vm((SUBS, ELEM_FIELDS * OWNED, BLK), BF16),
            pltpu.SemaphoreType.DMA((8 + BLK_DEV,)),
            pltpu.SemaphoreType.DMA((3 * SUBS,)),
        ],
        400_000_000,
        1_000_000,
        60,
    )(
        covariates, partition_slot, in_weight, in_bias[None], out_weight, out_bias,
        gradients, areas[None], corners.transpose(1, 0, 2), tile_rows[None], tile_cols[None], probe,
    )


def listed(everything):
    sds = jax.ShapeDtypeStruct
    return call(
        list_kernel,
        (
            sds((SLOTS, BLK), F32),
            sds((13, SLOTS, BLK), F32),
            sds((6, SLOTS, BLK), jnp.int32),
            sds((8, BLK), jnp.int32),
        ),
        [VMEM],
        (VMEM,) * 4,
        (),
        10_000_000,
        1_000_000,
    )(everything)


def finished(info, got, tid, geo, pos, before, own, after):
    vm = pltpu.VMEM
    return call(
        finish_kernel,
        jax.ShapeDtypeStruct((COLS, BLK_DEV * BLK), F32),
        [SMEM] + [VMEM] * 4 + [ANY] * 3,
        VMEM,
        [
            vm((BLK, RANKS * BLK), BF16),
            vm((6 * SLOTS, RANKS * BLK), BF16),
            vm((BLK, BLK), F32),
            vm((6, SLOTS, BLK), F32),
            vm((3 * SUBS * BLK_DEV, COLS, BLK), BF16),
            vm((BLK_DEV, COLS, BLK), F32),
            pltpu.SemaphoreType.DMA((3,)),
        ],
        1_000_000_000,
        3_000_000,
    )(info, got, tid, geo, pos, before, own, after)


def local(
    covariates,
    partition_slot,
    in_weight,
    in_bias,
    out_weight,
    out_bias,
    gradients,
    areas,
    corners,
    tile_rows,
    tile_cols,
    probe,
):
    slabs = lax.axis_size("slab")
    send = front(
        covariates, partition_slot, in_weight, in_bias, out_weight, out_bias,
        gradients, areas, corners, tile_rows, tile_cols, probe,
    )
    everything = lax.all_to_all(send, "sub", split_axis=0, concat_axis=0, tiled=True)
    routed = everything[:, :PROBE].transpose(1, 0, 2)
    got = lax.all_to_all(routed, "slab", split_axis=0, concat_axis=0, tiled=True)
    own = everything[:, PROBE:ELEMS].reshape(SUBS * BLK_DEV, COLS, BLK)
    up = [(i, i + 1) for i in range(slabs - 1)]
    before = lax.ppermute(own, "slab", up)
    after = lax.ppermute(own, "slab", [(j, i) for i, j in up])
    tid, geo, pos, info = listed(everything)
    return finished(info, got.reshape(-1, BLK), tid, geo, pos, before, own, after)


def solution(mesh):
    placed = (
        P(("slab", "sub"), None),
        P(None, ("slab", "sub")),
        P(),
        P(),
        P(),
        P(),
        P(None, None, ("slab", "sub")),
        P(("slab", "sub")),
        P(None, None, ("slab", "sub")),
        P(("slab", "sub")),
        P(("slab", "sub")),
        P(None, ("slab", "sub")),
    )
    return jax.shard_map(
        local, mesh=mesh, in_specs=placed, out_specs=P(None, ("slab", "sub")), check_vma=False
    )
```

```python
import jax
import jax.numpy as jnp
from jax import lax
from jax.experimental import pallas as pl
from jax.experimental.pallas import tpu as pltpu
from jax.sharding import PartitionSpec as P

BLK = 128
CHUNKS = 16
RANKS = 16
FIELDS = 8
SLOTS = 32
TILE_DEV = 16
SUBS = 4
BLK_DEV = 4
COLS = 64
PAIRS = ((0, 0), (0, 1), (0, 2), (1, 1), (1, 2), (2, 2))
PAIR_OF = {(a, b): PAIRS.index((min(a, b), max(a, b))) for a in range(3) for b in range(3)}
NT = (((1,), (1,)), ((), ()))
VMEM = pl.BlockSpec(memory_space=pltpu.VMEM)
SMEM = pl.BlockSpec(memory_space=pltpu.SMEM)
F32 = jnp.float32
BF16 = jnp.bfloat16
HBM = pl.BlockSpec(memory_space=pltpu.HBM)
OWNED = 8
ELEM_FIELDS = 18
PROBE = BLK
ELEMS = PROBE + BLK_DEV * COLS
SEND_ROWS = ELEMS + ELEM_FIELDS * OWNED
UNROLL = 16


def call(kernel, out_shape, in_specs, out_specs, scratch, flops, nbytes, vmem=40):
    return pl.pallas_call(
        kernel,
        out_shape=out_shape,
        in_specs=in_specs,
        out_specs=out_specs,
        scratch_shapes=scratch,
        compiler_params=pltpu.CompilerParams(vmem_limit_bytes=vmem * 1024 * 1024),
        cost_estimate=pl.CostEstimate(flops=flops, bytes_accessed=nbytes, transcendentals=0),
    )


def lanes(chunk):
    return slice(chunk * BLK, (chunk + 1) * BLK)


def halves(x):
    high = x.astype(BF16)
    return high, (x - high.astype(F32)).astype(BF16)


def start_all(pairs, sem):
    copies = [pltpu.make_async_copy(s, d, sem.at[i]) for i, (s, d) in enumerate(pairs)]
    for c in copies:
        c.start()
    return copies


def front_kernel(
    cov_hbm, slot_hbm, w1_hbm, b1_hbm, w2_hbm, b2_ref, grad_hbm, area_hbm, corner_hbm, rows_ref, cols_ref, probe_hbm,
    out_hbm,
    cov_ref, slot_ref, w1_ref, b1_ref, w2_ref, grad_ref, area_ref, corner_ref, tile_ref,
    hot_ref, rank_ref, val_ref, par_ref, send_ref, elem_ref, sem, out_sem,
):
    copies = start_all(
        (
            (slot_hbm, slot_ref), (grad_hbm, grad_ref), (area_hbm, area_ref), (corner_hbm, corner_ref),
            (w1_hbm, w1_ref), (b1_hbm, b1_ref), (w2_hbm, w2_ref), (cov_hbm, cov_ref),
            *(
                (probe_hbm.at[:, lanes(b)], send_ref.at[PROBE + b * COLS : PROBE + (b + 1) * COLS])
                for b in range(BLK_DEV)
            ),
        ),
        sem,
    )
    slab_iota = lax.broadcasted_iota(jnp.int32, (BLK, BLK), 0)
    lane_iota = lax.broadcasted_iota(jnp.int32, (BLK, BLK), 1)
    before = jnp.where(slab_iota < lane_iota, 1.0, 0.0).astype(BF16)
    earlier = jnp.concatenate([before, jnp.ones((BLK, BLK), BF16)], axis=1)
    tile_ref[...] = jnp.full(tile_ref.shape, -1.0, F32)
    tile_ref[0:1, 0:TILE_DEV] = rows_ref[...].astype(F32)
    tile_ref[1:2, 0:TILE_DEV] = cols_ref[...].astype(F32)
    row = tile_ref[0:1, :].astype(jnp.int32)
    col = tile_ref[1:2, :].astype(jnp.int32)
    real = lane_iota[0:1] < TILE_DEV
    owner = (row >> 2) & (SUBS - 1)
    mine = jnp.concatenate(
        [jnp.where(real & (owner == d), 1.0, 0.0) for d in range(SUBS)] + [jnp.zeros((12, BLK), F32)], axis=0
    )
    place = jnp.dot(mine.astype(BF16), before, preferred_element_type=F32)
    slot_iota = slab_iota[0:OWNED].astype(F32)
    pick = jnp.concatenate(
        [
            jnp.where((slot_iota == place[d : d + 1]) & (mine[d : d + 1] > 0.0), 1.0, 0.0)
            for d in range(SUBS)
        ],
        axis=0,
    ).astype(BF16)[:, :TILE_DEV]
    facts = [
        (lane_iota[0:1] + (lax.axis_index("sub") * TILE_DEV + 1)).astype(F32),
        (row & (BLK_DEV - 1)).astype(F32),
        (col >> 4).astype(F32),
        (col & 15).astype(F32),
    ]
    facts = jnp.concatenate([jnp.where(real, f, 0.0) for f in facts] + [jnp.zeros((BLK - 4, BLK), F32)], axis=0).T
    copies[0].wait()
    for chunk in range(CHUNKS):
        slab = slot_ref[0:1, lanes(chunk)] >> 2
        hot_ref[:, lanes(chunk)] = jnp.where(slab_iota == slab, 1.0, 0.0).astype(BF16)
    seen = jnp.zeros((BLK, BLK), F32)
    for chunk in range(CHUNKS):
        hot = hot_ref[:, lanes(chunk)]
        counts = jnp.dot(hot, earlier, preferred_element_type=F32)
        rank_ref[:, lanes(chunk)] = jnp.sum(
            hot.astype(F32) * (counts[:, :BLK] + seen), axis=0, keepdims=True
        )
        seen = seen + counts[:, BLK:]
    for c in copies[1:4]:
        c.wait()
    fields = []
    for v in range(5):
        value = area_ref[...] if v == 4 else grad_ref[v // 2, v % 2 : v % 2 + 1, :]
        fields += [half.astype(F32) for half in halves(value)]
    for side in range(2):
        for a in range(3):
            fields.append(corner_ref[a, side : side + 1, :].astype(F32))
    fields = [jnp.concatenate([f[:, lanes(k)] for k in range(TILE_DEV)], axis=0) for f in fields]
    fields += [facts[:TILE_DEV], jnp.zeros((TILE_DEV, BLK), F32)]
    picked = jnp.dot(pick, jnp.concatenate(fields, axis=1).astype(BF16), preferred_element_type=F32)
    for d in range(SUBS):
        elem_ref[d] = jnp.concatenate(
            [picked[d * OWNED : (d + 1) * OWNED, lanes(f)] for f in range(ELEM_FIELDS)], axis=0
        ).astype(BF16)
    for c in copies[8:]:
        c.wait()
    outs = start_all(
        [(send_ref.at[PROBE:], out_hbm.at[d, PROBE:ELEMS]) for d in range(SUBS)]
        + [(elem_ref.at[d], out_hbm.at[d, ELEMS:]) for d in range(SUBS)],
        out_sem,
    )
    for c in copies[4:8]:
        c.wait()
    rows = 512
    for part in range(cov_ref.shape[0] // rows):
        here = slice(part * rows, (part + 1) * rows)
        pre_act = jnp.dot(cov_ref[here, :], w1_ref[...], preferred_element_type=F32) + b1_ref[...]
        hidden = jax.nn.gelu(pre_act, approximate=True).astype(BF16)
        par_ref[:, here] = lax.dot_general(w2_ref[...], hidden, NT, preferred_element_type=F32)
    rank_iota = lax.broadcasted_iota(jnp.int32, (RANKS, BLK), 0).astype(F32)
    for chunk in range(CHUNKS):
        device = slot_ref[0:1, lanes(chunk)]
        place = slot_ref[1:2, lanes(chunk)]
        values = []
        for f in range(3):
            values += [half.astype(F32) for half in halves(par_ref[f : f + 1, lanes(chunk)] + b2_ref[f])]
        values += [((device & 3) * TILE_DEV + (place >> 7)).astype(F32), (place & 127).astype(F32)]
        ranked = rank_iota == rank_ref[:, lanes(chunk)]
        val_ref[:, lanes(chunk)] = jnp.concatenate(
            [jnp.where(ranked, v, 0.0).astype(BF16) for v in values], axis=0
        )
    send_ref[0:PROBE, :] = lax.dot_general(
        hot_ref[...], val_ref[...], NT, preferred_element_type=F32
    ).astype(BF16)
    last = [
        pltpu.make_async_copy(send_ref.at[:PROBE], out_hbm.at[d, :PROBE], out_sem.at[2 * SUBS + d])
        for d in range(SUBS)
    ]
    for c in last:
        c.start()
    for c in outs + last:
        c.wait()


def list_kernel(all_ref, tid_ref, geo_ref, pos_ref, info_ref):
    base = (lax.axis_index("slab") - 1) * (SUBS * BLK_DEV)
    sent = [all_ref[u, ELEMS:, :].astype(F32) for u in range(SUBS)]
    field = [
        jnp.concatenate([e[f * OWNED : (f + 1) * OWNED] for e in sent], axis=0) for f in range(ELEM_FIELDS - 1)
    ]
    facts = jnp.concatenate([field[16], jnp.zeros((BLK - SLOTS, BLK), F32)], axis=0)
    tid_ref[...] = jnp.broadcast_to(facts[:SLOTS, 0:1] - 1.0, (SLOTS, BLK))
    facts = facts.T
    col = (facts[2:3] * 16.0 + facts[3:4]).astype(jnp.int32) - base
    col = jnp.where(facts[0:1] > 0.0, col, SUBS * BLK_DEV)
    info_ref[...] = jnp.concatenate(
        [facts[1:2].astype(jnp.int32), col, jnp.zeros((6, BLK), jnp.int32)], axis=0
    )
    value = [field[2 * i] + field[2 * i + 1] for i in range(5)]
    grad_x = [value[0], value[1], -(value[0] + value[1])]
    grad_y = [value[2], value[3], -(value[2] + value[3])]
    for i, (a, b) in enumerate(PAIRS):
        geo_ref[i] = grad_x[a] * grad_x[b] + grad_y[a] * grad_y[b]
        geo_ref[6 + i] = grad_x[a] * grad_y[b] + grad_y[a] * grad_x[b]
    geo_ref[12] = value[4]
    for a in range(6):
        pos_ref[a] = field[10 + a].astype(jnp.int32)


def finish_kernel(
    info_ref, got_ref, tid_ref, geo_ref, pos_ref, before_ref, own_ref, after_ref,
    out_ref, hot_ref, val_ref, turned_ref, k_ref, acc_ref,
):
    blocks = SUBS * BLK_DEV
    lane_iota = lax.broadcasted_iota(jnp.int32, (BLK, BLK), 0).astype(F32).astype(BF16)
    one, zero = jnp.ones((), BF16), jnp.zeros((), BF16)
    tiles = tid_ref[...].astype(BF16)
    found = jnp.zeros((6 * SLOTS, BLK), F32)
    for u in range(SUBS):
        turned_ref[u] = got_ref[lanes(u), :].astype(F32).T
        for k in range(RANKS):
            rows = [
                jnp.broadcast_to(turned_ref[u, f * RANKS + k : f * RANKS + k + 1, :], (16, BLK)).astype(BF16)
                for f in range(FIELDS)
            ]
            twice = [jnp.concatenate([r, r], axis=0) for r in rows[:7]]
            mine = tiles == twice[6]
            val_ref[u, :, lanes(k)] = jnp.concatenate([jnp.where(mine, twice[f], zero) for f in range(6)], axis=0)
            hot_ref[u, :, lanes(k)] = jnp.where(lane_iota == jnp.concatenate([rows[7]] * 8, axis=0), one, zero)
        found = found + lax.dot_general(val_ref[u], hot_ref[u], NT, preferred_element_type=F32)
    params = [
        found[2 * f * SLOTS : (2 * f + 1) * SLOTS] + found[(2 * f + 1) * SLOTS : (2 * f + 2) * SLOTS]
        for f in range(3)
    ]
    kappa_sq = jnp.exp(params[0])
    scale = jnp.exp(params[1])
    coupling = 0.9 * jnp.tanh(params[2])
    area = geo_ref[12]
    for i, (a, b) in enumerate(PAIRS):
        mass = kappa_sq * (2.0 if a == b else 1.0)
        stiffness = scale * (geo_ref[i] + coupling * geo_ref[6 + i])
        k_ref[i] = (area * (stiffness + mass)).astype(BF16).astype(F32)
    acc_ref[...] = jnp.zeros(acc_ref.shape, F32)

    def tile_part(n):
        col = info_ref[1, n]
        at = col & (blocks - 1)
        x = jnp.where(
            col < blocks,
            before_ref[at].astype(F32),
            jnp.where(col < 2 * blocks, own_ref[at].astype(F32), after_ref[at].astype(F32)),
        )
        k = [k_ref[i, pl.ds(n, 1), :] for i in range(6)]
        xs = [
            jnp.take_along_axis(x, jnp.broadcast_to(pos_ref[3 + b, pl.ds(n, 1), :], (COLS, BLK)), axis=1)
            for b in range(3)
        ]
        ys = []
        hots = []
        for a in range(3):
            y = k[PAIR_OF[a, 0]] * xs[0] + k[PAIR_OF[a, 1]] * xs[1] + k[PAIR_OF[a, 2]] * xs[2]
            ys.append(y.astype(BF16))
            row = jnp.broadcast_to(pos_ref[a, pl.ds(n, 1), :].astype(F32), (16, BLK)).astype(BF16)
            hots.append(jnp.where(lane_iota == jnp.concatenate([row] * 8, axis=0), one, zero))
        return lax.dot_general(
            jnp.concatenate(ys, axis=1), jnp.concatenate(hots, axis=1), NT, preferred_element_type=F32
        )

    def add(group, carry):
        done = [tile_part(group * UNROLL + i) for i in range(UNROLL)]
        for i in range(UNROLL):
            block = info_ref[0, group * UNROLL + i]
            acc_ref[block] = acc_ref[block] + done[i]
        return carry

    lax.fori_loop(0, SLOTS // UNROLL, add, jnp.int32(0))
    for block in range(BLK_DEV):
        out_ref[:, lanes(block)] = acc_ref[block]


def front(covariates, partition_slot, in_weight, in_bias, out_weight, out_bias, gradients, areas, corners, tile_rows, tile_cols, probe):
    elements = areas.shape[0]
    vm = pltpu.VMEM
    return call(
        front_kernel,
        jax.ShapeDtypeStruct((SUBS, SEND_ROWS, BLK), BF16),
        [HBM] * 5 + [SMEM] + [HBM] * 3 + [VMEM] * 2 + [HBM],
        HBM,
        [
            vm(covariates.shape, BF16),
            vm(partition_slot.shape, jnp.int32),
            vm(in_weight.shape, BF16),
            vm((1, in_bias.shape[0]), F32),
            vm(out_weight.shape, BF16),
            vm(gradients.shape, F32),
            vm((1, elements), F32),
            vm((3, 2, elements), jnp.int32),
            vm((8, BLK), F32),
            vm((BLK, elements), BF16),
            vm((1, elements), F32),
            vm((BLK, elements), BF16),
            vm((3, elements), F32),
            vm((ELEMS, BLK), BF16),
            vm((SUBS, ELEM_FIELDS * OWNED, BLK), BF16),
            pltpu.SemaphoreType.DMA((8 + BLK_DEV,)),
            pltpu.SemaphoreType.DMA((3 * SUBS,)),
        ],
        400_000_000,
        1_000_000,
        60,
    )(
        covariates, partition_slot, in_weight, in_bias[None], out_weight, out_bias,
        gradients, areas[None], corners.transpose(1, 0, 2), tile_rows[None], tile_cols[None], probe,
    )


def listed(everything):
    sds = jax.ShapeDtypeStruct
    return call(
        list_kernel,
        (
            sds((SLOTS, BLK), F32),
            sds((13, SLOTS, BLK), F32),
            sds((6, SLOTS, BLK), jnp.int32),
            sds((8, BLK), jnp.int32),
        ),
        [VMEM],
        (VMEM,) * 4,
        (),
        10_000_000,
        1_000_000,
    )(everything)


def finished(info, got, tid, geo, pos, before, own, after):
    vm = pltpu.VMEM
    return call(
        finish_kernel,
        jax.ShapeDtypeStruct((COLS, BLK_DEV * BLK), F32),
        [SMEM] + [VMEM] * 7,
        VMEM,
        [
            vm((SUBS, BLK, RANKS * BLK), BF16),
            vm((SUBS, 6 * SLOTS, RANKS * BLK), BF16),
            vm((SUBS, BLK, BLK), F32),
            vm((6, SLOTS, BLK), F32),
            vm((BLK_DEV, COLS, BLK), F32),
        ],
        1_000_000_000,
        3_000_000,
    )(info, got, tid, geo, pos, before, own, after)


def local(
    covariates,
    partition_slot,
    in_weight,
    in_bias,
    out_weight,
    out_bias,
    gradients,
    areas,
    corners,
    tile_rows,
    tile_cols,
    probe,
):
    slabs = lax.axis_size("slab")
    send = front(
        covariates, partition_slot, in_weight, in_bias, out_weight, out_bias,
        gradients, areas, corners, tile_rows, tile_cols, probe,
    )
    everything = lax.all_to_all(send, "sub", split_axis=0, concat_axis=0, tiled=True)
    routed = everything[:, :PROBE].transpose(1, 0, 2)
    got = lax.all_to_all(routed, "slab", split_axis=0, concat_axis=0, tiled=True)
    own = everything[:, PROBE:ELEMS].reshape(SUBS * BLK_DEV, COLS, BLK)
    up = [(i, i + 1) for i in range(slabs - 1)]
    before = lax.ppermute(own, "slab", up)
    after = lax.ppermute(own, "slab", [(j, i) for i, j in up])
    tid, geo, pos, info = listed(everything)
    return finished(info, got.reshape(-1, BLK), tid, geo, pos, before, own, after)


def solution(mesh):
    placed = (
        P(("slab", "sub"), None),
        P(None, ("slab", "sub")),
        P(),
        P(),
        P(),
        P(),
        P(None, None, ("slab", "sub")),
        P(("slab", "sub")),
        P(None, None, ("slab", "sub")),
        P(("slab", "sub")),
        P(("slab", "sub")),
        P(None, ("slab", "sub")),
    )
    return jax.shard_map(
        local, mesh=mesh, in_specs=placed, out_specs=P(None, ("slab", "sub")), check_vma=False
    )
```

```python
import jax
import jax.numpy as jnp
from jax import lax
from jax.experimental import pallas as pl
from jax.experimental.pallas import tpu as pltpu
from jax.sharding import PartitionSpec as P

BLK = 128
CHUNKS = 16
RANKS = 16
FIELDS = 8
SLOTS = 32
TILE_DEV = 16
SUBS = 4
BLK_DEV = 4
COLS = 64
PAIRS = ((0, 0), (0, 1), (0, 2), (1, 1), (1, 2), (2, 2))
PAIR_OF = {(a, b): PAIRS.index((min(a, b), max(a, b))) for a in range(3) for b in range(3)}
NT = (((1,), (1,)), ((), ()))
VMEM = pl.BlockSpec(memory_space=pltpu.VMEM)
SMEM = pl.BlockSpec(memory_space=pltpu.SMEM)
F32 = jnp.float32
BF16 = jnp.bfloat16
HBM = pl.BlockSpec(memory_space=pltpu.HBM)
OWNED = 8
ELEM_FIELDS = 18
PROBE = BLK
ELEMS = PROBE + BLK_DEV * COLS
SEND_ROWS = ELEMS + ELEM_FIELDS * OWNED
UNROLL = 16


def call(kernel, out_shape, in_specs, out_specs, scratch, flops, nbytes, vmem=40):
    return pl.pallas_call(
        kernel,
        out_shape=out_shape,
        in_specs=in_specs,
        out_specs=out_specs,
        scratch_shapes=scratch,
        compiler_params=pltpu.CompilerParams(vmem_limit_bytes=vmem * 1024 * 1024),
        cost_estimate=pl.CostEstimate(flops=flops, bytes_accessed=nbytes, transcendentals=0),
    )


def lanes(chunk):
    return slice(chunk * BLK, (chunk + 1) * BLK)


def halves(x):
    high = x.astype(BF16)
    return high, (x - high.astype(F32)).astype(BF16)


def start_all(pairs, sem):
    copies = [pltpu.make_async_copy(s, d, sem.at[i]) for i, (s, d) in enumerate(pairs)]
    for c in copies:
        c.start()
    return copies


def front_kernel(
    cov_hbm, slot_hbm, w1_hbm, b1_hbm, w2_hbm, b2_ref, grad_hbm, area_hbm, corner_hbm, rows_ref, cols_ref, probe_hbm,
    out_ref,
    cov_ref, slot_ref, w1_ref, b1_ref, w2_ref, grad_ref, area_ref, corner_ref, tile_ref,
    hot_ref, rank_ref, val_ref, par_ref, sem,
):
    copies = start_all(
        (
            (slot_hbm, slot_ref), (grad_hbm, grad_ref), (area_hbm, area_ref), (corner_hbm, corner_ref),
            (w1_hbm, w1_ref), (b1_hbm, b1_ref), (w2_hbm, w2_ref), (cov_hbm, cov_ref),
            *(
                (probe_hbm.at[:, lanes(b)], out_ref.at[d, PROBE + b * COLS : PROBE + (b + 1) * COLS])
                for d in range(SUBS)
                for b in range(BLK_DEV)
            ),
        ),
        sem,
    )
    slab_iota = lax.broadcasted_iota(jnp.int32, (BLK, BLK), 0)
    lane_iota = lax.broadcasted_iota(jnp.int32, (BLK, BLK), 1)
    before = jnp.where(slab_iota < lane_iota, 1.0, 0.0).astype(BF16)
    earlier = jnp.concatenate([before, jnp.ones((BLK, BLK), BF16)], axis=1)
    tile_ref[...] = jnp.full(tile_ref.shape, -1.0, F32)
    tile_ref[0:1, 0:TILE_DEV] = rows_ref[...].astype(F32)
    tile_ref[1:2, 0:TILE_DEV] = cols_ref[...].astype(F32)
    row = tile_ref[0:1, :].astype(jnp.int32)
    col = tile_ref[1:2, :].astype(jnp.int32)
    real = lane_iota[0:1] < TILE_DEV
    owner = (row >> 2) & (SUBS - 1)
    mine = jnp.concatenate(
        [jnp.where(real & (owner == d), 1.0, 0.0) for d in range(SUBS)] + [jnp.zeros((12, BLK), F32)], axis=0
    )
    place = jnp.dot(mine.astype(BF16), before, preferred_element_type=F32)
    slot_iota = slab_iota[0:OWNED].astype(F32)
    pick = jnp.concatenate(
        [
            jnp.where((slot_iota == place[d : d + 1]) & (mine[d : d + 1] > 0.0), 1.0, 0.0)
            for d in range(SUBS)
        ],
        axis=0,
    ).astype(BF16)[:, :TILE_DEV]
    facts = [
        (lane_iota[0:1] + (lax.axis_index("sub") * TILE_DEV + 1)).astype(F32),
        (row & (BLK_DEV - 1)).astype(F32),
        (col >> 4).astype(F32),
        (col & 15).astype(F32),
    ]
    facts = jnp.concatenate([jnp.where(real, f, 0.0) for f in facts] + [jnp.zeros((BLK - 4, BLK), F32)], axis=0).T
    copies[0].wait()
    for chunk in range(CHUNKS):
        slab = slot_ref[0:1, lanes(chunk)] >> 2
        hot_ref[:, lanes(chunk)] = jnp.where(slab_iota == slab, 1.0, 0.0).astype(BF16)
    seen = jnp.zeros((BLK, BLK), F32)
    for chunk in range(CHUNKS):
        hot = hot_ref[:, lanes(chunk)]
        counts = jnp.dot(hot, earlier, preferred_element_type=F32)
        rank_ref[:, lanes(chunk)] = jnp.sum(
            hot.astype(F32) * (counts[:, :BLK] + seen), axis=0, keepdims=True
        )
        seen = seen + counts[:, BLK:]
    for c in copies[1:4]:
        c.wait()
    fields = []
    for v in range(5):
        value = area_ref[...] if v == 4 else grad_ref[v // 2, v % 2 : v % 2 + 1, :]
        fields += [half.astype(F32) for half in halves(value)]
    for side in range(2):
        for a in range(3):
            fields.append(corner_ref[a, side : side + 1, :].astype(F32))
    fields = [jnp.concatenate([f[:, lanes(k)] for k in range(TILE_DEV)], axis=0) for f in fields]
    fields += [facts[:TILE_DEV], jnp.zeros((TILE_DEV, BLK), F32)]
    picked = jnp.dot(pick, jnp.concatenate(fields, axis=1).astype(BF16), preferred_element_type=F32)
    for d in range(SUBS):
        out_ref[d, ELEMS:, :] = jnp.concatenate(
            [picked[d * OWNED : (d + 1) * OWNED, lanes(f)] for f in range(ELEM_FIELDS)], axis=0
        ).astype(BF16)
    for c in copies[4:8]:
        c.wait()
    rows = 512
    for part in range(cov_ref.shape[0] // rows):
        here = slice(part * rows, (part + 1) * rows)
        pre_act = jnp.dot(cov_ref[here, :], w1_ref[...], preferred_element_type=F32) + b1_ref[...]
        hidden = jax.nn.gelu(pre_act, approximate=True).astype(BF16)
        par_ref[:, here] = lax.dot_general(w2_ref[...], hidden, NT, preferred_element_type=F32)
    rank_iota = lax.broadcasted_iota(jnp.int32, (RANKS, BLK), 0).astype(F32)
    for chunk in range(CHUNKS):
        device = slot_ref[0:1, lanes(chunk)]
        place = slot_ref[1:2, lanes(chunk)]
        values = []
        for f in range(3):
            values += [half.astype(F32) for half in halves(par_ref[f : f + 1, lanes(chunk)] + b2_ref[f])]
        values += [((device & 3) * TILE_DEV + (place >> 7)).astype(F32), (place & 127).astype(F32)]
        ranked = rank_iota == rank_ref[:, lanes(chunk)]
        val_ref[:, lanes(chunk)] = jnp.concatenate(
            [jnp.where(ranked, v, 0.0).astype(BF16) for v in values], axis=0
        )
    routed = lax.dot_general(hot_ref[...], val_ref[...], NT, preferred_element_type=F32).astype(BF16)
    for d in range(SUBS):
        out_ref[d, 0:PROBE, :] = routed
    for c in copies[8:]:
        c.wait()


def list_kernel(all_ref, tid_ref, geo_ref, pos_ref, info_ref):
    base = (lax.axis_index("slab") - 1) * (SUBS * BLK_DEV)
    sent = [all_ref[u, ELEMS:, :].astype(F32) for u in range(SUBS)]
    field = [
        jnp.concatenate([e[f * OWNED : (f + 1) * OWNED] for e in sent], axis=0) for f in range(ELEM_FIELDS - 1)
    ]
    facts = jnp.concatenate([field[16], jnp.zeros((BLK - SLOTS, BLK), F32)], axis=0)
    tid_ref[...] = jnp.broadcast_to(facts[:SLOTS, 0:1] - 1.0, (SLOTS, BLK))
    facts = facts.T
    col = (facts[2:3] * 16.0 + facts[3:4]).astype(jnp.int32) - base
    col = jnp.where(facts[0:1] > 0.0, col, SUBS * BLK_DEV)
    info_ref[...] = jnp.concatenate(
        [facts[1:2].astype(jnp.int32), col, jnp.zeros((6, BLK), jnp.int32)], axis=0
    )
    value = [field[2 * i] + field[2 * i + 1] for i in range(5)]
    grad_x = [value[0], value[1], -(value[0] + value[1])]
    grad_y = [value[2], value[3], -(value[2] + value[3])]
    for i, (a, b) in enumerate(PAIRS):
        geo_ref[i] = grad_x[a] * grad_x[b] + grad_y[a] * grad_y[b]
        geo_ref[6 + i] = grad_x[a] * grad_y[b] + grad_y[a] * grad_x[b]
    geo_ref[12] = value[4]
    for a in range(6):
        pos_ref[a] = field[10 + a].astype(jnp.int32)


def finish_kernel(
    info_ref, got_ref, tid_ref, geo_ref, pos_ref, before_ref, own_ref, after_ref,
    out_ref, hot_ref, val_ref, turned_ref, k_ref, acc_ref,
):
    blocks = SUBS * BLK_DEV
    lane_iota = lax.broadcasted_iota(jnp.int32, (BLK, BLK), 0).astype(F32).astype(BF16)
    one, zero = jnp.ones((), BF16), jnp.zeros((), BF16)
    tiles = tid_ref[...].astype(BF16)
    found = jnp.zeros((6 * SLOTS, BLK), F32)
    for u in range(SUBS):
        turned_ref[u] = got_ref[lanes(u), :].astype(F32).T
        for k in range(RANKS):
            rows = [
                jnp.broadcast_to(turned_ref[u, f * RANKS + k : f * RANKS + k + 1, :], (16, BLK)).astype(BF16)
                for f in range(FIELDS)
            ]
            twice = [jnp.concatenate([r, r], axis=0) for r in rows[:7]]
            mine = tiles == twice[6]
            val_ref[u, :, lanes(k)] = jnp.concatenate([jnp.where(mine, twice[f], zero) for f in range(6)], axis=0)
            hot_ref[u, :, lanes(k)] = jnp.where(lane_iota == jnp.concatenate([rows[7]] * 8, axis=0), one, zero)
        found = found + lax.dot_general(val_ref[u], hot_ref[u], NT, preferred_element_type=F32)
    params = [
        found[2 * f * SLOTS : (2 * f + 1) * SLOTS] + found[(2 * f + 1) * SLOTS : (2 * f + 2) * SLOTS]
        for f in range(3)
    ]
    kappa_sq = jnp.exp(params[0])
    scale = jnp.exp(params[1])
    coupling = 0.9 * jnp.tanh(params[2])
    area = geo_ref[12]
    for i, (a, b) in enumerate(PAIRS):
        mass = kappa_sq * (2.0 if a == b else 1.0)
        stiffness = scale * (geo_ref[i] + coupling * geo_ref[6 + i])
        k_ref[i] = (area * (stiffness + mass)).astype(BF16).astype(F32)
    acc_ref[...] = jnp.zeros(acc_ref.shape, F32)

    def tile_part(n):
        col = info_ref[1, n]
        at = col & (blocks - 1)
        x = jnp.where(
            col < blocks,
            before_ref[at].astype(F32),
            jnp.where(col < 2 * blocks, own_ref[at].astype(F32), after_ref[at].astype(F32)),
        )
        k = [k_ref[i, pl.ds(n, 1), :] for i in range(6)]
        xs = [
            jnp.take_along_axis(x, jnp.broadcast_to(pos_ref[3 + b, pl.ds(n, 1), :], (COLS, BLK)), axis=1)
            for b in range(3)
        ]
        ys = []
        hots = []
        for a in range(3):
            y = k[PAIR_OF[a, 0]] * xs[0] + k[PAIR_OF[a, 1]] * xs[1] + k[PAIR_OF[a, 2]] * xs[2]
            ys.append(y.astype(BF16))
            row = jnp.broadcast_to(pos_ref[a, pl.ds(n, 1), :].astype(F32), (16, BLK)).astype(BF16)
            hots.append(jnp.where(lane_iota == jnp.concatenate([row] * 8, axis=0), one, zero))
        return lax.dot_general(
            jnp.concatenate(ys, axis=1), jnp.concatenate(hots, axis=1), NT, preferred_element_type=F32
        )

    def add(group, carry):
        done = [tile_part(group * UNROLL + i) for i in range(UNROLL)]
        for i in range(UNROLL):
            block = info_ref[0, group * UNROLL + i]
            acc_ref[block] = acc_ref[block] + done[i]
        return carry

    lax.fori_loop(0, SLOTS // UNROLL, add, jnp.int32(0))
    for block in range(BLK_DEV):
        out_ref[:, lanes(block)] = acc_ref[block]


def front(covariates, partition_slot, in_weight, in_bias, out_weight, out_bias, gradients, areas, corners, tile_rows, tile_cols, probe):
    elements = areas.shape[0]
    vm = pltpu.VMEM
    return call(
        front_kernel,
        jax.ShapeDtypeStruct((SUBS, SEND_ROWS, BLK), BF16),
        [HBM] * 5 + [SMEM] + [HBM] * 3 + [VMEM] * 2 + [HBM],
        VMEM,
        [
            vm(covariates.shape, BF16),
            vm(partition_slot.shape, jnp.int32),
            vm(in_weight.shape, BF16),
            vm((1, in_bias.shape[0]), F32),
            vm(out_weight.shape, BF16),
            vm(gradients.shape, F32),
            vm((1, elements), F32),
            vm((3, 2, elements), jnp.int32),
            vm((8, BLK), F32),
            vm((BLK, elements), BF16),
            vm((1, elements), F32),
            vm((BLK, elements), BF16),
            vm((3, elements), F32),
            pltpu.SemaphoreType.DMA((8 + SUBS * BLK_DEV,)),
        ],
        400_000_000,
        1_000_000,
        60,
    )(
        covariates, partition_slot, in_weight, in_bias[None], out_weight, out_bias,
        gradients, areas[None], corners.transpose(1, 0, 2), tile_rows[None], tile_cols[None], probe,
    )


def listed(everything):
    sds = jax.ShapeDtypeStruct
    return call(
        list_kernel,
        (
            sds((SLOTS, BLK), F32),
            sds((13, SLOTS, BLK), F32),
            sds((6, SLOTS, BLK), jnp.int32),
            sds((8, BLK), jnp.int32),
        ),
        [VMEM],
        (VMEM,) * 4,
        (),
        10_000_000,
        1_000_000,
    )(everything)


def finished(info, got, tid, geo, pos, before, own, after):
    vm = pltpu.VMEM
    return call(
        finish_kernel,
        jax.ShapeDtypeStruct((COLS, BLK_DEV * BLK), F32),
        [SMEM] + [VMEM] * 7,
        VMEM,
        [
            vm((SUBS, BLK, RANKS * BLK), BF16),
            vm((SUBS, 6 * SLOTS, RANKS * BLK), BF16),
            vm((SUBS, BLK, BLK), F32),
            vm((6, SLOTS, BLK), F32),
            vm((BLK_DEV, COLS, BLK), F32),
        ],
        1_000_000_000,
        3_000_000,
    )(info, got, tid, geo, pos, before, own, after)


def local(
    covariates,
    partition_slot,
    in_weight,
    in_bias,
    out_weight,
    out_bias,
    gradients,
    areas,
    corners,
    tile_rows,
    tile_cols,
    probe,
):
    slabs = lax.axis_size("slab")
    send = front(
        covariates, partition_slot, in_weight, in_bias, out_weight, out_bias,
        gradients, areas, corners, tile_rows, tile_cols, probe,
    )
    everything = lax.all_to_all(send, "sub", split_axis=0, concat_axis=0, tiled=True)
    routed = everything[:, :PROBE].transpose(1, 0, 2)
    got = lax.all_to_all(routed, "slab", split_axis=0, concat_axis=0, tiled=True)
    own = everything[:, PROBE:ELEMS].reshape(SUBS * BLK_DEV, COLS, BLK)
    up = [(i, i + 1) for i in range(slabs - 1)]
    before = lax.ppermute(own, "slab", up)
    after = lax.ppermute(own, "slab", [(j, i) for i, j in up])
    tid, geo, pos, info = listed(everything)
    return finished(info, got.reshape(-1, BLK), tid, geo, pos, before, own, after)


def solution(mesh):
    placed = (
        P(("slab", "sub"), None),
        P(None, ("slab", "sub")),
        P(),
        P(),
        P(),
        P(),
        P(None, None, ("slab", "sub")),
        P(("slab", "sub")),
        P(None, None, ("slab", "sub")),
        P(("slab", "sub")),
        P(("slab", "sub")),
        P(None, ("slab", "sub")),
    )
    return jax.shard_map(
        local, mesh=mesh, in_specs=placed, out_specs=P(None, ("slab", "sub")), check_vma=False
    )
```
